256 devices in a mesh: pipe: 16 (over z, x_lo), expert: 16 (over x_hi, y, core).
Axes of the slice: x: 4 (x_hi: 2, x_lo: 2; x = x_hi * 2 + x_lo), y: 4, z: 8, core: 2. Of those that a mesh axis runs over, the one named last changes fastest.
Arguments:
- forward_in: bfloat16 [16, 256, 7168], P('pipe', 'expert'), may hold values from -6 to 6
- forward_route: int32 [16, 256], P('pipe', 'expert'), may hold values from 0 to 1, as said below
- backward_in: bfloat16 [16, 256, 7168], P('pipe', 'expert'), may hold values from -6 to 6
- backward_route: int32 [16, 256], P('pipe', 'expert'), may hold values from 0 to 1, as said below
- backward_grad: bfloat16 [16, 256, 7168], P('pipe', 'expert'), may hold values from -6 to 6
- router: bfloat16 [16, 7168, 2], P('pipe'), may hold values from -0.125 to 0.125
- gate_weight: bfloat16 [16, 7168, 4096], P('pipe', None, 'expert'), may hold values from -0.0625 to 0.0625
- up_weight: bfloat16 [16, 7168, 4096], P('pipe', None, 'expert'), may hold values from -0.0625 to 0.0625
- down_weight: bfloat16 [16, 4096, 7168], P('pipe', 'expert'), may hold values from -0.125 to 0.125
Outputs:
- forward_next: bfloat16 [16, 256, 7168], P('pipe', 'expert')
- backward_out: bfloat16 [16, 256, 7168], P('pipe', 'expert')
The draws below stay inside these ranges and needn't reach their ends.
Inputs may be any that keep to these rules, and one draw needn't show every extreme that they name: `forward_route`: in every section's micro-batch each expert is named by exactly 128 tokens. `backward_route`: in every section's micro-batch each expert is named by exactly 128 tokens.
All inputs are finite; a program needn't handle non-finite values.
Results may differ from the reference program's by a relative error of at most 0.014.
Values may be sent and summed in bfloat16 or wider, within the bound.
No kernel may reach another device: no remote copies, remote signals or barrier semaphores. Data moves between devices by JAX's collectives and lax.ppermute only.
A program may use at most 128 MiB of HBM per device.

```python
import jax
import jax.numpy as jnp
from jax import lax

D = 7168
FF = 2048
EXPERTS = 2
SECTIONS = 16
TOKENS = 256


def balanced_routes(key):
    base = jnp.arange(TOKENS, dtype=jnp.int32) % EXPERTS
    table = jnp.broadcast_to(base[None, :], (SECTIONS, TOKENS))
    return jax.random.permutation(key, table, axis=1, independent=True).astype(jnp.int32)


def draw_forward_route(key, part):
    key = jax.random.fold_in(key, 11)
    return balanced_routes(key)


def draw_backward_route(key, part):
    key = jax.random.fold_in(key, 23)
    return balanced_routes(key)


def levels(stream_key, dims, shards, smallest, top_value):
    def one(dim, parts):
        steps = jax.random.uniform(jax.random.fold_in(jax.random.fold_in(stream_key, 6), dim), (parts,), jnp.float32, smallest / len(shards), top_value / len(shards))
        return jnp.repeat(jnp.exp(steps), dims[dim] // parts).reshape((-1,) + (1,) * (len(dims) - dim - 1))

    level = one(*shards[0])
    for cut in shards[1:]:
        level = level * one(*cut)
    return level


def scatter_about(own_key, shape, deviation, limit, split=(), held_as=jnp.bfloat16):
    values = deviation * jax.random.normal(own_key, shape, jnp.float32)
    if split:
        values = values * levels(own_key, shape, split, -0.22, 0.18)
    return jnp.clip(values, -limit, limit).astype(held_as)


def setup_inputs(seed: int = 0) -> dict:
    arg_keys = jax.random.split(jax.random.key(seed), 10)
    return {
        "forward_in": scatter_about(arg_keys[0], (SECTIONS, TOKENS, D), 1.0, 6.0, ((0, 16), (1, 16))),
        "forward_route": draw_forward_route(jax.random.fold_in(arg_keys[9], 71), 0),
        "backward_in": scatter_about(arg_keys[2], (SECTIONS, TOKENS, D), 1.0, 6.0, ((0, 16), (1, 16))),
        "backward_route": draw_backward_route(jax.random.fold_in(arg_keys[9], 71), 0),
        "backward_grad": scatter_about(arg_keys[4], (SECTIONS, TOKENS, D), 1.0, 6.0, ((0, 16), (1, 16))),
        "router": scatter_about(arg_keys[5], (SECTIONS, D, EXPERTS), (D // 4) ** -0.5, 0.125, ((0, 16),)),
        "gate_weight": scatter_about(arg_keys[6], (SECTIONS, D, EXPERTS * FF), D ** -0.5, 0.0625, ((0, 16), (2, 16))),
        "up_weight": scatter_about(arg_keys[7], (SECTIONS, D, EXPERTS * FF), D ** -0.5, 0.0625, ((0, 16), (2, 16))),
        "down_weight": scatter_about(arg_keys[8], (SECTIONS, EXPERTS * FF, D), FF ** -0.5, 0.125, ((0, 16), (1, 16))),
    }


def silu_slope(values):
    logistic = jax.nn.sigmoid(values)
    return logistic * (1.0 + values * (1.0 - logistic))


def choose(routes, number):
    return (routes[:, None] == jnp.arange(number, dtype=jnp.int32)[None, :]).astype(jnp.float32)


def section_pass(pieces):
    forward_in, forward_route, backward_in, backward_route, backward_grad, router, gate_weight, up_weight, down_weight = pieces
    selected = choose(forward_route, EXPERTS)
    logits = jnp.dot(forward_in, router, preferred_element_type=jnp.float32)
    gate_values = jax.nn.sigmoid(jnp.sum(logits * selected, axis=1))
    mixture = jnp.zeros((TOKENS, D), jnp.float32)
    for expert in range(EXPERTS):
        gate_cols = gate_weight[:, expert * FF:(expert + 1) * FF]
        up_cols = up_weight[:, expert * FF:(expert + 1) * FF]
        down_rows = down_weight[expert * FF:(expert + 1) * FF]
        gate_pre = jnp.dot(forward_in, gate_cols, preferred_element_type=jnp.float32)
        up_pre = jnp.dot(forward_in, up_cols, preferred_element_type=jnp.float32)
        hidden = (jax.nn.silu(gate_pre) * up_pre * selected[:, expert:expert + 1]).astype(jnp.bfloat16)
        mixture = mixture + jnp.dot(hidden, down_rows, preferred_element_type=jnp.float32)
    section_out = (forward_in.astype(jnp.float32) + gate_values[:, None] * mixture).astype(jnp.bfloat16)

    chosen = choose(backward_route, EXPERTS)
    back_logits = jnp.dot(backward_in, router, preferred_element_type=jnp.float32)
    back_gates = jax.nn.sigmoid(jnp.sum(back_logits * chosen, axis=1))
    scaled = (back_gates[:, None] * backward_grad.astype(jnp.float32)).astype(jnp.bfloat16)
    through = jnp.zeros((TOKENS, D), jnp.float32)
    weight_sum = jnp.zeros((TOKENS,), jnp.float32)
    for expert in range(EXPERTS):
        gate_cols = gate_weight[:, expert * FF:(expert + 1) * FF]
        up_cols = up_weight[:, expert * FF:(expert + 1) * FF]
        down_rows = down_weight[expert * FF:(expert + 1) * FF]
        row_mask = chosen[:, expert:expert + 1]
        gate_pre = jnp.dot(backward_in, gate_cols, preferred_element_type=jnp.float32)
        up_pre = jnp.dot(backward_in, up_cols, preferred_element_type=jnp.float32)
        activated = jax.nn.silu(gate_pre)
        hidden = (activated * up_pre * row_mask).astype(jnp.bfloat16)
        down_slope = jnp.dot(scaled, down_rows.T, preferred_element_type=jnp.float32) * row_mask
        weight_sum = weight_sum + jnp.sum(hidden.astype(jnp.float32) * down_slope, axis=1)
        gate_slope = (down_slope * up_pre * silu_slope(gate_pre)).astype(jnp.bfloat16)
        up_slope = (down_slope * activated).astype(jnp.bfloat16)
        through = through + jnp.dot(gate_slope, gate_cols.T, preferred_element_type=jnp.float32)
        through = through + jnp.dot(up_slope, up_cols.T, preferred_element_type=jnp.float32)
    router_rows = jnp.dot(chosen, router.astype(jnp.float32).T, precision=lax.Precision.HIGHEST)
    section_grad = (backward_grad.astype(jnp.float32) + through + (weight_sum * (1.0 - back_gates))[:, None] * router_rows).astype(jnp.bfloat16)
    return section_out, section_grad


def reference(forward_in, forward_route, backward_in, backward_route, backward_grad, router, gate_weight, up_weight, down_weight):
    section_out, section_grad = lax.map(section_pass, (forward_in, forward_route, backward_in, backward_route, backward_grad, router, gate_weight, up_weight, down_weight))
    return jnp.roll(section_out, 1, axis=0), jnp.roll(section_grad, -1, axis=0)
```

```python
import jax
import jax.numpy as jnp
from jax import lax
from jax.sharding import PartitionSpec as P

COLUMNS = 2
CHIPS = 4
CORES = 2
F32 = jnp.float32
BF16 = jnp.bfloat16


def place(column, chip, core):
    return (column * CHIPS + chip % CHIPS) * CORES + core


def moved(block, step):
    pairs = []
    for column in range(COLUMNS):
        for chip in range(CHIPS):
            for core in range(CORES):
                pairs.append((place(column, chip, core), place(*step(column, chip, core))))
    return lax.ppermute(block, "expert", pairs)


def other_column(block):
    return moved(block, lambda column, chip, core: (1 - column, chip, core))


def chip_up(block):
    return moved(block, lambda column, chip, core: (column, chip + 1, core))


def chip_down(block):
    return moved(block, lambda column, chip, core: (column, chip - 1, core))


def other_core(block):
    return moved(block, lambda column, chip, core: (column, chip, 1 - core))


def to_home(block, distance, cross):
    sections = lax.axis_size("pipe")
    width = COLUMNS * CHIPS * CORES
    pairs = []
    for section in range(sections):
        there = (section + distance) % sections
        for column in range(COLUMNS):
            for chip in range(CHIPS):
                for core in range(CORES):
                    target = 1 - column if cross else column
                    pairs.append(
                        (
                            section * width + place(column, chip, core),
                            there * width + place(target, chip, core),
                        )
                    )
    return lax.ppermute(block, ("pipe", "expert"), pairs)


def collect(block):
    rows = block.shape[0]
    both = jnp.concatenate([block, other_column(block)], axis=0)
    below = chip_up(both)
    above = chip_down(both)
    first = chip_up(below[:rows])
    second = chip_down(above[rows:])
    return jnp.concatenate([both, below, above, first, second], axis=0)


def give_back(mine, other):
    total = mine.astype(F32) + other_core(other).astype(F32)
    rows = total.shape[0] // CHIPS
    half = rows // 2
    own, below, above, opposite = (total[i * rows : (i + 1) * rows] for i in range(CHIPS))
    opposite = opposite.astype(BF16)
    first = chip_down(opposite[:half])
    second = chip_up(opposite[half:])
    below = jnp.concatenate([below[:half] + first.astype(F32), below[half:]], axis=0)
    above = jnp.concatenate([above[:half], above[half:] + second.astype(F32)], axis=0)
    from_above = chip_down(below.astype(BF16))
    from_below = chip_up(above.astype(BF16))
    return own + from_above.astype(F32) + from_below.astype(F32)


def silu_slope(values):
    logistic = jax.nn.sigmoid(values)
    return logistic * (1.0 + values * (1.0 - logistic))


def dot(left, right):
    return jnp.dot(left, right, preferred_element_type=F32)


def dot_turned(left, right):
    return lax.dot_general(left, right, (((1,), (1,)), ((), ())), preferred_element_type=F32)


def on_device(
    forward_in,
    forward_route,
    backward_in,
    backward_route,
    backward_grad,
    router,
    gate_weight,
    up_weight,
    down_weight,
):
    gate_local = gate_weight[0]
    up_local = up_weight[0]
    down_local = down_weight[0]
    rows = forward_in.shape[1]
    column = lax.axis_index("expert") // (CHIPS * CORES)
    router_mine = jnp.where(column == 0, router[0][:, 0], router[0][:, 1])

    routes = collect(jnp.stack([forward_route[0], backward_route[0]], axis=1))
    routes_other = other_core(routes)
    forward_mask, backward_mask = (
        (routes[:, i : i + 1] == column).astype(F32) for i in range(2)
    )
    forward_mask_other, backward_mask_other = (
        (routes_other[:, i : i + 1] == column).astype(F32) for i in range(2)
    )

    def gates_of(x):
        return jax.nn.sigmoid(dot(x, router_mine[:, None]))

    def forward_part(x, mask):
        hidden = jax.nn.silu(dot(x, gate_local)) * dot(x, up_local) * mask
        return (gates_of(x) * dot(hidden.astype(BF16), down_local)).astype(BF16)

    def backward_part(x, grad, mask):
        gates = gates_of(x)
        gate_pre = dot(x, gate_local)
        up_pre = dot(x, up_local)
        activated = jax.nn.silu(gate_pre)
        hidden = (activated * up_pre * mask).astype(BF16)
        down_slope = dot_turned(grad, down_local) * (gates * mask)
        weight = jnp.sum(hidden.astype(F32) * down_slope, axis=1, keepdims=True)
        gate_slope = (down_slope * up_pre * silu_slope(gate_pre)).astype(BF16)
        up_slope = (down_slope * activated).astype(BF16)
        through = dot_turned(gate_slope, gate_local) + dot_turned(up_slope, up_local)
        return (through + (weight * (1.0 - gates)) * router_mine.astype(F32)[None, :]).astype(BF16)

    def finish(base, summed, mask, distance):
        out = (base.astype(F32) * mask + summed).astype(BF16)
        return to_home(out[:rows], distance, False) + to_home(out[rows:], distance, True)

    forward_rows = collect(forward_in[0])
    forward_other = other_core(forward_rows)
    backward_rows = collect(backward_in[0])
    gradient_rows = collect(backward_grad[0])
    backward_other = other_core(backward_rows)
    gradient_other = other_core(gradient_rows)

    part_other = forward_part(forward_other, forward_mask_other)
    part = forward_part(forward_rows, forward_mask)
    forward_sum = give_back(part, part_other)
    own = 2 * rows
    forward_next = finish(forward_rows[:own], forward_sum, forward_mask[:own], 1)

    part_other = backward_part(backward_other, gradient_other, backward_mask_other)
    part = backward_part(backward_rows, gradient_rows, backward_mask)
    backward_sum = give_back(part, part_other)
    backward_out = finish(gradient_rows[:own], backward_sum, backward_mask[:own], -1)
    return (forward_next[None], backward_out[None])


def solution(mesh):
    return jax.shard_map(
        on_device,
        mesh=mesh,
        in_specs=(
            P("pipe", "expert", None),
            P("pipe", "expert"),
            P("pipe", "expert", None),
            P("pipe", "expert"),
            P("pipe", "expert", None),
            P("pipe", None, None),
            P("pipe", None, "expert"),
            P("pipe", None, "expert"),
            P("pipe", "expert", None),
        ),
        out_specs=(P("pipe", "expert", None), P("pipe", "expert", None)),
        check_vma=False,
    )
```

```python
import functools

import jax
import jax.numpy as jnp
from jax import lax
from jax.experimental import pallas as pl
from jax.experimental.pallas import tpu as pltpu
from jax.sharding import PartitionSpec as P

COLUMNS = 2
CHIPS = 4
CORES = 2
TILE = 1024
LANES = 128
F32 = jnp.float32
BF16 = jnp.bfloat16


def place(column, chip, core):
    return (column * CHIPS + chip % CHIPS) * CORES + core


def moved(block, step):
    pairs = []
    for column in range(COLUMNS):
        for chip in range(CHIPS):
            for core in range(CORES):
                pairs.append((place(column, chip, core), place(*step(column, chip, core))))
    return lax.ppermute(block, "expert", pairs)


def other_column(block):
    return moved(block, lambda column, chip, core: (1 - column, chip, core))


def other_core(block):
    return moved(block, lambda column, chip, core: (column, chip, 1 - core))


def onward(block):
    return moved(block, lambda column, chip, core: (column, chip + 1 - 2 * core, core))


def backward(block):
    return moved(block, lambda column, chip, core: (column, chip - 1 + 2 * core, core))


def to_home(block, distance, cross):
    sections = lax.axis_size("pipe")
    width = COLUMNS * CHIPS * CORES
    pairs = []
    for section in range(sections):
        there = (section + distance) % sections
        for column in range(COLUMNS):
            for chip in range(CHIPS):
                for core in range(CORES):
                    target = 1 - column if cross else column
                    pairs.append(
                        (
                            section * width + place(column, chip, core),
                            there * width + place(target, chip, core),
                        )
                    )
    return lax.ppermute(block, ("pipe", "expert"), pairs)


def collect(own, cross):
    piece = jnp.concatenate([own, other_column(cross)], axis=0)
    pieces, swapped = [piece], [other_core(piece)]
    for _ in range(CHIPS - 1):
        piece = onward(piece)
        pieces.append(piece)
        swapped.append(other_core(piece))
    return pieces, swapped


def give_back(mine, other):
    total = None
    for j in reversed(range(CHIPS)):
        both = mine[j].astype(F32) + other_core(other[j]).astype(F32)
        if total is not None:
            both = both + backward(total.astype(BF16)).astype(F32)
        total = both
    return total


def dot(left, right):
    return jnp.dot(left, right, preferred_element_type=F32)


def dot_turned(left, right):
    return lax.dot_general(left, right, (((1,), (1,)), ((), ())), preferred_element_type=F32)


def lane_sums(x, row):
    total = jnp.zeros((x.shape[0], LANES), F32)
    for start in range(0, x.shape[1], LANES):
        part = x[:, start : start + LANES].astype(F32)
        total = total + part * row[:, start : start + LANES]
    return total


def sigmoid(values):
    return 1.0 / (1.0 + jnp.exp(-values))


def forward_kernel(count, steps, *refs):
    x_refs = refs[:count]
    gate_ref, up_ref, down_ref, router_ref = refs[count : count + 4]
    out_refs = refs[count + 4 : 2 * count + 4]
    gate_acc, up_acc, logit_acc, hidden, gates = refs[2 * count + 4 :]
    i = pl.program_id(0)

    @pl.when(i == 0)
    def _():
        gate_acc[...] = jnp.zeros_like(gate_acc)
        up_acc[...] = jnp.zeros_like(up_acc)
        logit_acc[...] = jnp.zeros_like(logit_acc)

    @pl.when(i < steps)
    def _():
        x = jnp.concatenate([ref[...] for ref in x_refs], axis=0)
        gate_acc[...] += dot(x, gate_ref[...])
        up_acc[...] += dot(x, up_ref[...])
        logit_acc[...] += lane_sums(x, router_ref[...])

    @pl.when(i == steps)
    def _():
        gates[...] = sigmoid(jnp.sum(logit_acc[...], axis=1, keepdims=True))
        gate_pre = gate_acc[...]
        hidden[...] = (gate_pre * sigmoid(gate_pre) * up_acc[...]).astype(BF16)

    @pl.when(i >= steps)
    def _():
        part = (gates[...] * dot(hidden[...], down_ref[...])).astype(BF16)
        rows = part.shape[0] // count
        for j, ref in enumerate(out_refs):
            ref[...] = part[j * rows : (j + 1) * rows]


def backward_kernel(count, steps, *refs):
    x_refs = refs[:count]
    gate_ref, up_ref, down_ref, router_ref = refs[count : count + 4]
    out_refs = refs[count + 4 : 2 * count + 4]
    gate_acc, up_acc, down_acc, logit_acc, gate_slope, up_slope, weight = refs[2 * count + 4 :]
    i = pl.program_id(0)

    @pl.when(i == 0)
    def _():
        gate_acc[...] = jnp.zeros_like(gate_acc)
        up_acc[...] = jnp.zeros_like(up_acc)
        down_acc[...] = jnp.zeros_like(down_acc)
        logit_acc[...] = jnp.zeros_like(logit_acc)

    @pl.when(i < steps)
    def _():
        rows = x_refs[0].shape[0] // 2
        x = jnp.concatenate([ref[:rows] for ref in x_refs], axis=0)
        grad = jnp.concatenate([ref[rows:] for ref in x_refs], axis=0)
        gate_acc[...] += dot(x, gate_ref[...])
        up_acc[...] += dot(x, up_ref[...])
        down_acc[...] += dot_turned(grad, down_ref[...])
        logit_acc[...] += lane_sums(x, router_ref[...])

    @pl.when(i == steps)
    def _():
        gates = sigmoid(jnp.sum(logit_acc[...], axis=1, keepdims=True))
        gate_pre = gate_acc[...]
        up_pre = up_acc[...]
        logistic = sigmoid(gate_pre)
        activated = gate_pre * logistic
        down_slope = gates * down_acc[...]
        hidden = (activated * up_pre).astype(BF16).astype(F32)
        weight[...] = jnp.sum(hidden * down_slope, axis=1, keepdims=True) * (1.0 - gates)
        slope = logistic * (1.0 + gate_pre * (1.0 - logistic))
        gate_slope[...] = (down_slope * up_pre * slope).astype(BF16)
        up_slope[...] = (down_slope * activated).astype(BF16)

    @pl.when(i >= steps)
    def _():
        through = dot_turned(gate_slope[...], gate_ref[...])
        through += dot_turned(up_slope[...], up_ref[...])
        part = (through + weight[...] * router_ref[...]).astype(BF16)
        rows = part.shape[0] // count
        for j, ref in enumerate(out_refs):
            ref[...] = part[j * rows : (j + 1) * rows]


def expert_parts(pieces, gate, up, down, router_row, is_backward):
    model, hidden_units = gate.shape
    steps = model // TILE
    count = len(pieces)
    per_piece = pieces[0].shape[0]
    token_rows = per_piece // 2 if is_backward else per_piece
    rows = token_rows * count

    def first(i):
        return jnp.minimum(i, steps - 1)

    def second(i):
        return jnp.maximum(i - steps, 0)

    def both(i):
        return lax.rem(i, steps)

    if is_backward:
        body = functools.partial(backward_kernel, count, steps)
        weight_at, down_at, router_at = both, first, both
        scratch = [
            pltpu.VMEM((rows, hidden_units), F32),
            pltpu.VMEM((rows, hidden_units), F32),
            pltpu.VMEM((rows, hidden_units), F32),
            pltpu.VMEM((rows, LANES), F32),
            pltpu.VMEM((rows, hidden_units), BF16),
            pltpu.VMEM((rows, hidden_units), BF16),
            pltpu.VMEM((rows, 1), F32),
        ]
    else:
        body = functools.partial(forward_kernel, count, steps)
        weight_at, down_at, router_at = first, second, first
        scratch = [
            pltpu.VMEM((rows, hidden_units), F32),
            pltpu.VMEM((rows, hidden_units), F32),
            pltpu.VMEM((rows, LANES), F32),
            pltpu.VMEM((rows, hidden_units), BF16),
            pltpu.VMEM((rows, 1), F32),
        ]
    products = 5 if is_backward else 3
    return pl.pallas_call(
        body,
        grid=(2 * steps,),
        in_specs=[pl.BlockSpec((per_piece, TILE), lambda i: (0, first(i)))] * count
        + [
            pl.BlockSpec((TILE, hidden_units), lambda i: (weight_at(i), 0)),
            pl.BlockSpec((TILE, hidden_units), lambda i: (weight_at(i), 0)),
            pl.BlockSpec((hidden_units, TILE), lambda i: (0, down_at(i))),
            pl.BlockSpec((1, TILE), lambda i: (0, router_at(i))),
        ],
        out_specs=[pl.BlockSpec((token_rows, TILE), lambda i: (0, second(i)))] * count,
        out_shape=[jax.ShapeDtypeStruct((token_rows, model), BF16)] * count,
        scratch_shapes=scratch,
        compiler_params=pltpu.CompilerParams(vmem_limit_bytes=32 * 1024 * 1024),
        cost_estimate=pl.CostEstimate(
            flops=products * 2 * rows * model * hidden_units,
            bytes_accessed=(products * hidden_units + 2 * rows) * model * 2,
            transcendentals=rows * hidden_units,
        ),
    )(*pieces, gate, up, down, router_row)


def on_device(
    forward_in,
    forward_route,
    backward_in,
    backward_route,
    backward_grad,
    router,
    gate_weight,
    up_weight,
    down_weight,
):
    weights = gate_weight[0], up_weight[0], down_weight[0]
    rows = forward_in.shape[1]
    column = lax.axis_index("expert") // (CHIPS * CORES)
    router_row = jnp.where(column == 0, router[0][:, 0], router[0][:, 1]).astype(F32)[None, :]

    def split(block, route):
        mine = route[0][:, None] == column
        nothing = jnp.zeros((), block.dtype)
        return jnp.where(mine, block[0], nothing), jnp.where(mine, nothing, block[0])

    def finish(base, summed, distance):
        out = (base.astype(F32) + summed).astype(BF16)
        return to_home(out[:rows], distance, False) + to_home(out[rows:], distance, True)

    own, cross = split(forward_in, forward_route)
    forward_rows, forward_swapped = collect(own, cross)
    x_own, x_cross = split(backward_in, backward_route)
    grad_own, grad_cross = split(backward_grad, backward_route)
    arrived = other_column(jnp.concatenate([x_cross, grad_cross], axis=0))
    piece = jnp.concatenate([x_own, arrived[:rows], grad_own, arrived[rows:]], axis=0)
    backward_rows, backward_swapped = [piece], [other_core(piece)]
    for _ in range(CHIPS - 1):
        piece = onward(piece)
        backward_rows.append(piece)
        backward_swapped.append(other_core(piece))

    parts = expert_parts(forward_rows + forward_swapped, *weights, router_row, False)
    forward_sum = give_back(parts[:CHIPS], parts[CHIPS:])
    forward_next = finish(forward_rows[0], forward_sum, 1)

    parts = expert_parts(backward_rows + backward_swapped, *weights, router_row, True)
    backward_sum = give_back(parts[:CHIPS], parts[CHIPS:])
    backward_out = finish(backward_rows[0][2 * rows :], backward_sum, -1)
    return (forward_next[None], backward_out[None])


def solution(mesh):
    return jax.shard_map(
        on_device,
        mesh=mesh,
        in_specs=(
            P("pipe", "expert", None),
            P("pipe", "expert"),
            P("pipe", "expert", None),
            P("pipe", "expert"),
            P("pipe", "expert", None),
            P("pipe", None, None),
            P("pipe", None, "expert"),
            P("pipe", None, "expert"),
            P("pipe", "expert", None),
        ),
        out_specs=(P("pipe", "expert", None), P("pipe", "expert", None)),
        check_vma=False,
    )
```

```python
import functools

import jax
import jax.numpy as jnp
from jax import lax
from jax.experimental import pallas as pl
from jax.experimental.pallas import tpu as pltpu
from jax.sharding import PartitionSpec as P

COLUMNS = 2
CHIPS = 4
CORES = 2
TILE = 1792
LANES = 128
F32 = jnp.float32
BF16 = jnp.bfloat16


def place(column, chip, core):
    return (column * CHIPS + chip % CHIPS) * CORES + core


def moved(block, step):
    pairs = []
    for column in range(COLUMNS):
        for chip in range(CHIPS):
            for core in range(CORES):
                pairs.append((place(column, chip, core), place(*step(column, chip, core))))
    return lax.ppermute(block, "expert", pairs)


def join(*blocks):
    return lax.optimization_barrier(blocks)


def other_column(block):
    return moved(block, lambda column, chip, core: (1 - column, chip, core))


def other_core(block):
    return moved(block, lambda column, chip, core: (column, chip, 1 - core))


def onward(block):
    return moved(block, lambda column, chip, core: (column, chip + 1 - 2 * core, core))


def backward(block):
    return moved(block, lambda column, chip, core: (column, chip - 1 + 2 * core, core))


def to_home(block, distance, cross):
    sections = lax.axis_size("pipe")
    width = COLUMNS * CHIPS * CORES
    pairs = []
    for section in range(sections):
        there = (section + distance) % sections
        for column in range(COLUMNS):
            for chip in range(CHIPS):
                for core in range(CORES):
                    target = 1 - column if cross else column
                    pairs.append(
                        (
                            section * width + place(column, chip, core),
                            there * width + place(target, chip, core),
                        )
                    )
    return lax.ppermute(block, ("pipe", "expert"), pairs)


def summed(mine, *others):
    total = mine.astype(F32)
    for other in others:
        total = total + other.astype(F32)
    return total


def dot(left, right):
    return jnp.dot(left, right, preferred_element_type=F32)


def dot_turned(left, right):
    return lax.dot_general(left, right, (((1,), (1,)), ((), ())), preferred_element_type=F32)


def lane_sums(x, row):
    total = jnp.zeros((x.shape[0], LANES), F32)
    for start in range(0, x.shape[1], LANES):
        part = x[:, start : start + LANES].astype(F32)
        total = total + part * row[:, start : start + LANES]
    return total


def sigmoid(values):
    return 1.0 / (1.0 + jnp.exp(-values))


def forward_kernel(count, steps, *refs):
    x_refs, route_refs = refs[:count], refs[count : 2 * count]
    gate_ref, up_ref, down_ref, router_ref, column_ref = refs[2 * count : 2 * count + 5]
    out_refs = refs[2 * count + 5 : 3 * count + 5]
    gate_acc, up_acc, logit_acc, hidden, gates = refs[3 * count + 5 :]
    i = pl.program_id(0)

    @pl.when(i == 0)
    def _():
        gate_acc[...] = jnp.zeros_like(gate_acc)
        up_acc[...] = jnp.zeros_like(up_acc)
        logit_acc[...] = jnp.zeros_like(logit_acc)

    @pl.when(i < steps)
    def _():
        x = jnp.concatenate([ref[...] for ref in x_refs], axis=0)
        gate_acc[...] += dot(x, gate_ref[...])
        up_acc[...] += dot(x, up_ref[...])
        logit_acc[...] += lane_sums(x, router_ref[...])

    @pl.when(i == steps)
    def _():
        gates[...] = sigmoid(jnp.sum(logit_acc[...], axis=1, keepdims=True))
        routes = jnp.concatenate([ref[...] for ref in route_refs], axis=0).astype(F32)
        mask = (routes == column_ref[...]).astype(F32)
        mask = jnp.concatenate([mask] * (hidden.shape[1] // LANES), axis=1)
        gate_pre = gate_acc[...]
        hidden[...] = (gate_pre * sigmoid(gate_pre) * up_acc[...] * mask).astype(BF16)

    @pl.when(i >= steps)
    def _():
        part = (gates[...] * dot(hidden[...], down_ref[...])).astype(BF16)
        rows = part.shape[0] // count
        for j, ref in enumerate(out_refs):
            ref[...] = part[j * rows : (j + 1) * rows]


def backward_kernel(count, steps, *refs):
    x_refs = refs[:count]
    gate_ref, up_ref, down_ref, router_ref = refs[count : count + 4]
    out_refs = refs[count + 4 : 2 * count + 4]
    gate_acc, up_acc, down_acc, logit_acc, gate_slope, up_slope, weight = refs[2 * count + 4 :]
    i = pl.program_id(0)

    @pl.when(i == 0)
    def _():
        gate_acc[...] = jnp.zeros_like(gate_acc)
        up_acc[...] = jnp.zeros_like(up_acc)
        down_acc[...] = jnp.zeros_like(down_acc)
        logit_acc[...] = jnp.zeros_like(logit_acc)

    @pl.when(i < steps)
    def _():
        rows = x_refs[0].shape[0] // 2
        x = jnp.concatenate([ref[:rows] for ref in x_refs], axis=0)
        grad = jnp.concatenate([ref[rows:] for ref in x_refs], axis=0)
        gate_acc[...] += dot(x, gate_ref[...])
        up_acc[...] += dot(x, up_ref[...])
        down_acc[...] += dot_turned(grad, down_ref[...])
        logit_acc[...] += lane_sums(x, router_ref[...])

    @pl.when(i == steps)
    def _():
        gates = sigmoid(jnp.sum(logit_acc[...], axis=1, keepdims=True))
        gate_pre = gate_acc[...]
        up_pre = up_acc[...]
        logistic = sigmoid(gate_pre)
        activated = gate_pre * logistic
        down_slope = gates * down_acc[...]
        hidden = (activated * up_pre).astype(BF16).astype(F32)
        weight[...] = jnp.sum(hidden * down_slope, axis=1, keepdims=True) * (1.0 - gates)
        slope = logistic * (1.0 + gate_pre * (1.0 - logistic))
        gate_slope[...] = (down_slope * up_pre * slope).astype(BF16)
        up_slope[...] = (down_slope * activated).astype(BF16)

    @pl.when(i >= steps)
    def _():
        through = dot_turned(gate_slope[...], gate_ref[...])
        through += dot_turned(up_slope[...], up_ref[...])
        part = (through + weight[...] * router_ref[...]).astype(BF16)
        rows = part.shape[0] // count
        for j, ref in enumerate(out_refs):
            ref[...] = part[j * rows : (j + 1) * rows]


def expert_parts(pieces, gate, up, down, router_row, column_row, is_backward):
    model, hidden_units = gate.shape
    steps = model // TILE
    count = len(pieces)
    per_piece = pieces[0].shape[0]
    token_rows = per_piece // 2 if is_backward else per_piece
    rows = token_rows * count

    def first(i):
        return jnp.minimum(i, steps - 1)

    def second(i):
        return jnp.maximum(i - steps, 0)

    def both(i):
        return lax.rem(i, steps)

    if is_backward:
        body = functools.partial(backward_kernel, count, steps)
        weight_at, down_at, router_at = both, first, both
        scratch = [
            pltpu.VMEM((rows, hidden_units), F32),
            pltpu.VMEM((rows, hidden_units), F32),
            pltpu.VMEM((rows, hidden_units), F32),
            pltpu.VMEM((rows, LANES), F32),
            pltpu.VMEM((rows, hidden_units), BF16),
            pltpu.VMEM((rows, hidden_units), BF16),
            pltpu.VMEM((rows, 1), F32),
        ]
    else:
        body = functools.partial(forward_kernel, count, steps)
        weight_at, down_at, router_at = first, second, first
        scratch = [
            pltpu.VMEM((rows, hidden_units), F32),
            pltpu.VMEM((rows, hidden_units), F32),
            pltpu.VMEM((rows, LANES), F32),
            pltpu.VMEM((rows, hidden_units), BF16),
            pltpu.VMEM((rows, 1), F32),
        ]
    products = 5 if is_backward else 3
    route_specs = [pl.BlockSpec((per_piece, LANES), lambda i: (0, model // LANES))] * count
    gate, up, down = (
        pltpu.with_memory_space_constraint(weight, pltpu.HBM) for weight in (gate, up, down)
    )
    return pl.pallas_call(
        body,
        grid=(2 * steps,),
        in_specs=[pl.BlockSpec((per_piece, TILE), lambda i: (0, first(i)))] * count
        + ([] if is_backward else route_specs)
        + [
            pl.BlockSpec((TILE, hidden_units), lambda i: (weight_at(i), 0)),
            pl.BlockSpec((TILE, hidden_units), lambda i: (weight_at(i), 0)),
            pl.BlockSpec((hidden_units, TILE), lambda i: (0, down_at(i))),
            pl.BlockSpec((1, TILE), lambda i: (0, router_at(i))),
        ]
        + ([] if is_backward else [pl.BlockSpec((1, LANES), lambda i: (0, 0))]),
        out_specs=[pl.BlockSpec((token_rows, TILE), lambda i: (0, second(i)))] * count,
        out_shape=[jax.ShapeDtypeStruct((token_rows, model), BF16)] * count,
        scratch_shapes=scratch,
        compiler_params=pltpu.CompilerParams(vmem_limit_bytes=24 * 1024 * 1024),
        cost_estimate=pl.CostEstimate(
            flops=products * 2 * rows * model * hidden_units,
            bytes_accessed=(products * hidden_units + 2 * rows) * model * 2,
            transcendentals=rows * hidden_units,
        ),
    )(
        *pieces,
        *([] if is_backward else pieces),
        gate,
        up,
        down,
        router_row,
        *([] if is_backward else [column_row]),
    )


def on_device(
    forward_in,
    forward_route,
    backward_in,
    backward_route,
    backward_grad,
    router,
    gate_weight,
    up_weight,
    down_weight,
):
    weights = gate_weight[0], up_weight[0], down_weight[0]
    rows = forward_in.shape[1]
    column = lax.axis_index("expert") // (CHIPS * CORES)
    router_row = jnp.where(column == 0, router[0][:, 0], router[0][:, 1]).astype(F32)[None, :]

    column_row = jnp.full((1, LANES), column, F32)

    def split(block, route):
        mine = route[0][:, None] == column
        nothing = jnp.zeros((), block.dtype)
        return jnp.where(mine, block[0], nothing), jnp.where(mine, nothing, block[0])

    def stack(*blocks):
        return jnp.concatenate(blocks, axis=0)

    x_own, x_cross = split(backward_in, backward_route)
    grad_own, grad_cross = split(backward_grad, backward_route)
    lanes = jnp.broadcast_to(forward_route[0].astype(BF16)[:, None], (rows, LANES))
    f0 = jnp.concatenate([forward_in[0], lanes], axis=1)

    x_arrived, f1 = join(other_column(x_cross), onward(f0))
    f1, grad_cross = join(f1, grad_cross)
    grad_arrived, f2 = join(other_column(grad_cross), onward(f1))
    b0 = stack(x_own, x_arrived, grad_own, grad_arrived)
    near = stack(f0, f1)
    b0, near, f2 = join(b0, near, f2)
    b1, near_crossed, f3 = join(onward(b0), other_column(near), onward(f2))
    far = stack(f2, f3)
    b1, far = join(b1, far)
    b2, far_crossed = join(onward(b1), other_column(far))
    pieces = [near, far, near_crossed, far_crossed]
    pieces = pieces + [other_core(piece) for piece in pieces]
    b2, *pieces = join(b2, *pieces)
    parts = expert_parts(pieces, *weights, router_row, column_row, False)
    b3, *parts = join(onward(b2), *parts)

    far_back = summed(parts[3], other_core(parts[7])).astype(BF16)
    pieces = [b0, b1, b2, b3]
    pieces = pieces + [other_core(piece) for piece in pieces]
    far_back, *pieces = join(far_back, *pieces)
    near_back = summed(parts[2], other_core(parts[6])).astype(BF16)
    far_here = summed(parts[1], other_core(parts[5]))
    near_here = summed(parts[0], other_core(parts[4]))
    b_parts = expert_parts(pieces, *weights, router_row, column_row, True)
    far_back, near_back, *b_parts = join(other_column(far_back), near_back, *b_parts)

    far_here = summed(far_here, far_back)
    b_total = summed(b_parts[3], other_core(b_parts[7])).astype(BF16)
    f_total = far_here[rows:].astype(BF16)
    near_back, b_total, f_total = join(near_back, b_total, f_total)
    near_back, f_total = other_column(near_back), backward(f_total)
    b_total = summed(backward(b_total), b_parts[2], other_core(b_parts[6])).astype(BF16)
    b_total = summed(backward(b_total), b_parts[1], other_core(b_parts[5])).astype(BF16)
    b_total, near_back, f_total = join(b_total, near_back, f_total)
    near_here = summed(near_here, near_back)
    f_total = summed(f_total, far_here[:rows]).astype(BF16)
    b_total, f_total = join(backward(b_total), backward(f_total))
    b_total = summed(b_total, b_parts[0], other_core(b_parts[4]), b0[2 * rows :]).astype(BF16)
    f_total = summed(f_total, near_here[rows:]).astype(BF16)
    b_total, f_total = join(b_total, f_total)
    f_total = summed(backward(f_total), near_here[:rows], forward_in[0]).astype(BF16)
    forward_next = to_home(f_total, 1, False)
    backward_out = to_home(b_total[:rows], -1, False) + to_home(b_total[rows:], -1, True)
    return (forward_next[None], backward_out[None])


def solution(mesh):
    return jax.shard_map(
        on_device,
        mesh=mesh,
        in_specs=(
            P("pipe", "expert", None),
            P("pipe", "expert"),
            P("pipe", "expert", None),
            P("pipe", "expert"),
            P("pipe", "expert", None),
            P("pipe", None, None),
            P("pipe", None, "expert"),
            P("pipe", None, "expert"),
            P("pipe", "expert", None),
        ),
        out_specs=(P("pipe", "expert", None), P("pipe", "expert", None)),
        check_vma=False,
    )
```

```python
import functools

import jax
import jax.numpy as jnp
from jax import lax
from jax.experimental import pallas as pl
from jax.experimental.pallas import tpu as pltpu
from jax.sharding import PartitionSpec as P

COLUMNS = 2
CHIPS = 4
CORES = 2
TILE = 1792
LANES = 128
F32 = jnp.float32
BF16 = jnp.bfloat16


def place(column, chip, core):
    return (column * CHIPS + chip % CHIPS) * CORES + core


def moved(block, step):
    pairs = []
    for column in range(COLUMNS):
        for chip in range(CHIPS):
            for core in range(CORES):
                pairs.append((place(column, chip, core), place(*step(column, chip, core))))
    return lax.ppermute(block, "expert", pairs)


def join(*blocks):
    return lax.optimization_barrier(blocks)


def other_column(block):
    return moved(block, lambda column, chip, core: (1 - column, chip, core))


def other_core(block):
    return moved(block, lambda column, chip, core: (column, chip, 1 - core))


def onward(block):
    return moved(block, lambda column, chip, core: (column, chip + 1 - 2 * core, core))


def backward(block):
    return moved(block, lambda column, chip, core: (column, chip - 1 + 2 * core, core))


def opposite(block):
    return moved(block, lambda column, chip, core: (column, chip + 2, core))


def after(block, *others):
    return lax.optimization_barrier((block, *others))[0]


def to_home(block, distance, cross):
    sections = lax.axis_size("pipe")
    width = COLUMNS * CHIPS * CORES
    pairs = []
    for section in range(sections):
        there = (section + distance) % sections
        for column in range(COLUMNS):
            for chip in range(CHIPS):
                for core in range(CORES):
                    target = 1 - column if cross else column
                    pairs.append(
                        (
                            section * width + place(column, chip, core),
                            there * width + place(target, chip, core),
                        )
                    )
    return lax.ppermute(block, ("pipe", "expert"), pairs)


def summed(mine, *others):
    total = mine.astype(F32)
    for other in others:
        total = total + other.astype(F32)
    return total


def dot(left, right):
    return jnp.dot(left, right, preferred_element_type=F32)


def dot_turned(left, right):
    return lax.dot_general(left, right, (((1,), (1,)), ((), ())), preferred_element_type=F32)


def lane_sums(x, row):
    total = jnp.zeros((x.shape[0], LANES), F32)
    for start in range(0, x.shape[1], LANES):
        part = x[:, start : start + LANES].astype(F32)
        total = total + part * row[:, start : start + LANES]
    return total


def sigmoid(values):
    return 1.0 / (1.0 + jnp.exp(-values))


def store(part, out_refs):
    start = 0
    for ref in out_refs:
        rows = ref.shape[0]
        ref[...] = part[start : start + rows]
        start += rows


def forward_kernel(count, steps, *refs):
    x_refs, route_refs = refs[:count], refs[count : 2 * count]
    gate_ref, up_ref, down_ref, router_ref, column_ref = refs[2 * count : 2 * count + 5]
    out_refs = refs[2 * count + 5 : -5]
    gate_acc, up_acc, logit_acc, hidden, gates = refs[-5:]
    i = pl.program_id(0)

    @pl.when(i == 0)
    def _():
        gate_acc[...] = jnp.zeros_like(gate_acc)
        up_acc[...] = jnp.zeros_like(up_acc)
        logit_acc[...] = jnp.zeros_like(logit_acc)

    @pl.when(i < steps)
    def _():
        x = jnp.concatenate([ref[...] for ref in x_refs], axis=0)
        gate_acc[...] += dot(x, gate_ref[...])
        up_acc[...] += dot(x, up_ref[...])
        logit_acc[...] += lane_sums(x, router_ref[...])

    @pl.when(i == steps)
    def _():
        gates[...] = sigmoid(jnp.sum(logit_acc[...], axis=1, keepdims=True))
        routes = jnp.concatenate([ref[...] for ref in route_refs], axis=0).astype(F32)
        mask = (routes == column_ref[...]).astype(F32)
        mask = jnp.concatenate([mask] * (hidden.shape[1] // LANES), axis=1)
        gate_pre = gate_acc[...]
        hidden[...] = (gate_pre * sigmoid(gate_pre) * up_acc[...] * mask).astype(BF16)

    @pl.when(i >= steps)
    def _():
        part = (gates[...] * dot(hidden[...], down_ref[...])).astype(BF16)
        store(part, out_refs)


def backward_kernel(count, steps, *refs):
    x_refs, grad_refs = refs[:count], refs[count : 2 * count]
    gate_ref, up_ref, down_ref, router_ref = refs[2 * count : 2 * count + 4]
    out_refs = refs[2 * count + 4 : -7]
    gate_acc, up_acc, down_acc, logit_acc, gate_slope, up_slope, weight = refs[-7:]
    i = pl.program_id(0)

    @pl.when(i == 0)
    def _():
        gate_acc[...] = jnp.zeros_like(gate_acc)
        up_acc[...] = jnp.zeros_like(up_acc)
        down_acc[...] = jnp.zeros_like(down_acc)
        logit_acc[...] = jnp.zeros_like(logit_acc)

    @pl.when(i < steps)
    def _():
        x = jnp.concatenate([ref[...] for ref in x_refs], axis=0)
        grad = jnp.concatenate([ref[...] for ref in grad_refs], axis=0)
        gate_acc[...] += dot(x, gate_ref[...])
        up_acc[...] += dot(x, up_ref[...])
        down_acc[...] += dot_turned(grad, down_ref[...])
        logit_acc[...] += lane_sums(x, router_ref[...])

    @pl.when(i == steps)
    def _():
        gates = sigmoid(jnp.sum(logit_acc[...], axis=1, keepdims=True))
        gate_pre = gate_acc[...]
        up_pre = up_acc[...]
        logistic = sigmoid(gate_pre)
        activated = gate_pre * logistic
        down_slope = gates * down_acc[...]
        hidden = (activated * up_pre).astype(BF16).astype(F32)
        weight[...] = jnp.sum(hidden * down_slope, axis=1, keepdims=True) * (1.0 - gates)
        slope = logistic * (1.0 + gate_pre * (1.0 - logistic))
        gate_slope[...] = (down_slope * up_pre * slope).astype(BF16)
        up_slope[...] = (down_slope * activated).astype(BF16)

    @pl.when(i >= steps)
    def _():
        through = dot_turned(gate_slope[...], gate_ref[...])
        through += dot_turned(up_slope[...], up_ref[...])
        part = (through + weight[...] * router_ref[...]).astype(BF16)
        store(part, out_refs)


def expert_parts(pieces, grads, out_rows, gate, up, down, router_row, column_row):
    is_backward = grads is not None
    model, hidden_units = gate.shape
    steps = model // TILE
    count = len(pieces)
    per_piece = pieces[0].shape[0]
    rows = per_piece * count

    def first(i):
        return jnp.minimum(i, steps - 1)

    def second(i):
        return jnp.maximum(i - steps, 0)

    def both(i):
        return lax.rem(i, steps)

    if is_backward:
        body = functools.partial(backward_kernel, count, steps)
        weight_at, down_at, router_at = both, first, both
        scratch = [
            pltpu.VMEM((rows, hidden_units), F32),
            pltpu.VMEM((rows, hidden_units), F32),
            pltpu.VMEM((rows, hidden_units), F32),
            pltpu.VMEM((rows, LANES), F32),
            pltpu.VMEM((rows, hidden_units), BF16),
            pltpu.VMEM((rows, hidden_units), BF16),
            pltpu.VMEM((rows, 1), F32),
        ]
    else:
        body = functools.partial(forward_kernel, count, steps)
        weight_at, down_at, router_at = first, second, first
        scratch = [
            pltpu.VMEM((rows, hidden_units), F32),
            pltpu.VMEM((rows, hidden_units), F32),
            pltpu.VMEM((rows, LANES), F32),
            pltpu.VMEM((rows, hidden_units), BF16),
            pltpu.VMEM((rows, 1), F32),
        ]
    products = 5 if is_backward else 3
    x_specs = [pl.BlockSpec((per_piece, TILE), lambda i: (0, first(i)))] * count
    route_specs = [pl.BlockSpec((per_piece, LANES), lambda i: (0, model // LANES))] * count
    gate, up, down = (
        pltpu.with_memory_space_constraint(weight, pltpu.HBM) for weight in (gate, up, down)
    )
    return pl.pallas_call(
        body,
        grid=(2 * steps,),
        in_specs=x_specs + (x_specs if is_backward else route_specs)
        + [
            pl.BlockSpec((TILE, hidden_units), lambda i: (weight_at(i), 0)),
            pl.BlockSpec((TILE, hidden_units), lambda i: (weight_at(i), 0)),
            pl.BlockSpec((hidden_units, TILE), lambda i: (0, down_at(i))),
            pl.BlockSpec((1, TILE), lambda i: (0, router_at(i))),
        ]
        + ([] if is_backward else [pl.BlockSpec((1, LANES), lambda i: (0, 0))]),
        out_specs=[pl.BlockSpec((n, TILE), lambda i: (0, second(i))) for n in out_rows],
        out_shape=[jax.ShapeDtypeStruct((n, model), BF16) for n in out_rows],
        scratch_shapes=scratch,
        compiler_params=pltpu.CompilerParams(vmem_limit_bytes=24 * 1024 * 1024),
        cost_estimate=pl.CostEstimate(
            flops=products * 2 * rows * model * hidden_units,
            bytes_accessed=(products * hidden_units + 2 * rows) * model * 2,
            transcendentals=rows * hidden_units,
        ),
    )(
        *pieces,
        *(grads if is_backward else pieces),
        gate,
        up,
        down,
        router_row,
        *([] if is_backward else [column_row]),
    )


def on_device(
    forward_in,
    forward_route,
    backward_in,
    backward_route,
    backward_grad,
    router,
    gate_weight,
    up_weight,
    down_weight,
):
    weights = gate_weight[0], up_weight[0], down_weight[0]
    rows = forward_in.shape[1]
    column = lax.axis_index("expert") // (CHIPS * CORES)
    router_row = jnp.where(column == 0, router[0][:, 0], router[0][:, 1]).astype(F32)[None, :]

    column_row = jnp.full((1, LANES), column, F32)

    def split(block, route):
        mine = route[0][:, None] == column
        nothing = jnp.zeros((), block.dtype)
        return jnp.where(mine, block[0], nothing), jnp.where(mine, nothing, block[0])

    def stack(*blocks):
        return jnp.concatenate(blocks, axis=0)

    x_own, x_cross = split(backward_in, backward_route)
    grad_own, grad_cross = split(backward_grad, backward_route)
    lanes = jnp.broadcast_to(forward_route[0].astype(BF16)[:, None], (rows, LANES))
    f0 = jnp.concatenate([forward_in[0], lanes], axis=1)

    x_arrived = other_column(x_cross)
    f1, f3, f2 = onward(f0), backward(f0), opposite(f0)
    grad_arrived = other_column(grad_cross)
    x0 = stack(x_own, x_arrived)
    x1 = onward(x0)
    here = stack(f0, f1, f2, f3)
    crossed = other_column(after(here, x0))
    g0 = stack(grad_own, after(grad_arrived, here))
    g1 = onward(g0)
    x2 = onward(after(x1, g0))
    g2 = onward(after(g1, x1))
    x3_from = after(x2, g1)
    x3 = onward(x3_from)
    g3_from = after(g2, x2)
    g3 = onward(g3_from)
    pieces = [here, crossed, other_core(here), other_core(crossed)]
    pieces[-1] = after(pieces[-1], x3_from, g3_from)
    parts = expert_parts(pieces, None, [4 * rows] * 4, *weights, router_row, column_row)
    x3, g3, *parts = join(x3, g3, *parts)

    cross_sum = summed(parts[1], other_core(parts[3])).astype(BF16)
    far_back = cross_sum[2 * rows :]
    xs, gs = [x0, x1, x2, x3], [g0, g1, g2, g3]
    xs = xs + [other_core(x) for x in xs]
    gs = gs + [other_core(g) for g in gs]
    far_back, xs[-1], gs[-1] = join(far_back, xs[-1], gs[-1])
    b_parts = expert_parts(
        xs, gs, [rows] * 8 + [4 * rows] * 2, *weights, router_row, column_row
    )
    far_back, near_back, *b_parts = join(other_column(far_back), cross_sum[: 2 * rows], *b_parts)

    b_other = [other_core(b_parts[9]), other_core(b_parts[8])]

    def of_piece(j, cross):
        start = ((j % 2) * 2 + cross) * rows
        return b_parts[2 * j + cross], b_other[0 if j >= 2 else 1][start : start + rows]

    own3 = summed(*of_piece(3, 0)).astype(BF16)
    cross3 = summed(*of_piece(3, 1)).astype(BF16)
    own3, cross3, near_back = join(own3, cross3, near_back)
    own2, cross2, near_back = backward(own3), backward(cross3), other_column(near_back)
    own2 = summed(own2, *of_piece(2, 0)).astype(BF16)
    cross2 = summed(after(cross2, own2), *of_piece(2, 1)).astype(BF16)
    own1, cross1 = backward(own2), backward(cross2)
    near_back = after(near_back, cross2)
    f_sum = summed(parts[0], other_core(parts[2]), stack(near_back, far_back))
    f_send = f_sum.astype(BF16)
    f_back = [
        backward(f_send[rows : 2 * rows]),
        opposite(f_send[2 * rows : 3 * rows]),
        onward(f_send[3 * rows :]),
    ]
    own1 = summed(after(own1, f_send), *of_piece(1, 0)).astype(BF16)
    cross1 = summed(after(cross1, own1), *of_piece(1, 1)).astype(BF16)
    own0, cross0 = backward(own1), backward(cross1)
    f_total = summed(f_sum[:rows], after(forward_in[0], cross1), *f_back).astype(BF16)
    own0 = summed(after(own0, f_total), *of_piece(0, 0), grad_own).astype(BF16)
    cross0 = summed(after(cross0, own0), *of_piece(0, 1), g0[rows:]).astype(BF16)
    forward_next = to_home(f_total, 1, False)
    own_home = to_home(own0, -1, False)
    cross_home = to_home(cross0, -1, True)
    return (forward_next[None], (own_home + cross_home)[None])


def solution(mesh):
    return jax.shard_map(
        on_device,
        mesh=mesh,
        in_specs=(
            P("pipe", "expert", None),
            P("pipe", "expert"),
            P("pipe", "expert", None),
            P("pipe", "expert"),
            P("pipe", "expert", None),
            P("pipe", None, None),
            P("pipe", None, "expert"),
            P("pipe", None, "expert"),
            P("pipe", "expert", None),
        ),
        out_specs=(P("pipe", "expert", None), P("pipe", "expert", None)),
        check_vma=False,
    )
```

```python
import functools

import jax
import jax.numpy as jnp
from jax import lax
from jax.experimental import pallas as pl
from jax.experimental.pallas import tpu as pltpu
from jax.sharding import PartitionSpec as P

COLUMNS = 2
CHIPS = 4
CORES = 2
TILE = 1024
LANES = 128
F32 = jnp.float32
BF16 = jnp.bfloat16


def place(column, chip, core):
    return (column * CHIPS + chip % CHIPS) * CORES + core


def moved(block, step):
    pairs = []
    for column in range(COLUMNS):
        for chip in range(CHIPS):
            for core in range(CORES):
                pairs.append((place(column, chip, core), place(*step(column, chip, core))))
    return lax.ppermute(block, "expert", pairs)


def join(*blocks):
    return lax.optimization_barrier(blocks)


def other_column(block):
    return moved(block, lambda column, chip, core: (1 - column, chip, core))


def other_core(block):
    return moved(block, lambda column, chip, core: (column, chip, 1 - core))


def onward(block):
    return moved(block, lambda column, chip, core: (column, chip + 1 - 2 * core, core))


def backward(block):
    return moved(block, lambda column, chip, core: (column, chip - 1 + 2 * core, core))


def opposite(block):
    return moved(block, lambda column, chip, core: (column, chip + 2, core))


def after(block, *others):
    return lax.optimization_barrier((block, *others))[0]


def to_home(block, distance, cross):
    sections = lax.axis_size("pipe")
    width = COLUMNS * CHIPS * CORES
    pairs = []
    for section in range(sections):
        there = (section + distance) % sections
        for column in range(COLUMNS):
            for chip in range(CHIPS):
                for core in range(CORES):
                    target = 1 - column if cross else column
                    pairs.append(
                        (
                            section * width + place(column, chip, core),
                            there * width + place(target, chip, core),
                        )
                    )
    return lax.ppermute(block, ("pipe", "expert"), pairs)


def summed(mine, *others):
    total = mine.astype(F32)
    for other in others:
        total = total + other.astype(F32)
    return total


def dot(left, right):
    return jnp.dot(left, right, preferred_element_type=F32)


def dot_turned(left, right):
    return lax.dot_general(left, right, (((1,), (1,)), ((), ())), preferred_element_type=F32)


def lane_sums(x, row):
    total = jnp.zeros((x.shape[0], LANES), F32)
    for start in range(0, x.shape[1], LANES):
        part = x[:, start : start + LANES].astype(F32)
        total = total + part * row[:, start : start + LANES]
    return total


def sigmoid(values):
    return 1.0 / (1.0 + jnp.exp(-values))


def cuts(size):
    return [slice(start, start + TILE) for start in range(0, size, TILE)]


def stacked(refs, cut):
    return jnp.concatenate([ref[:, cut] for ref in refs], axis=0)


def interleaved(refs, cut):
    rows = refs[0].shape[0] // CHIPS
    blocks = []
    for own, cross in (refs[:2], refs[2:]):
        for start in range(0, CHIPS * rows, rows):
            blocks.extend([own[start : start + rows, cut], cross[start : start + rows, cut]])
    return jnp.concatenate(blocks, axis=0)


def store(part, out_refs, cut):
    start = 0
    for ref in out_refs:
        rows = ref.shape[0]
        ref[:, cut] = part[start : start + rows]
        start += rows


def forward_kernel(count, *refs):
    x_refs = refs[:count]
    gate_ref, up_ref, down_ref, router_ref, column_ref = refs[count : count + 5]
    out_refs = refs[count + 5 :]
    model, hidden_units = gate_ref.shape
    rows = count * x_refs[0].shape[0]
    gate_pre = jnp.zeros((rows, hidden_units), F32)
    up_pre = jnp.zeros((rows, hidden_units), F32)
    logits = jnp.zeros((rows, LANES), F32)
    for cut in cuts(model):
        x = interleaved(x_refs, cut)
        logits += lane_sums(x, router_ref[:, cut])
        gate_pre += dot(x, gate_ref[cut, :])
        up_pre += dot(x, up_ref[cut, :])
    gates = sigmoid(jnp.sum(logits, axis=1, keepdims=True))
    routes = interleaved(x_refs, slice(model, model + LANES)).astype(F32)
    mask = (routes == column_ref[...]).astype(F32)
    mask = jnp.concatenate([mask] * (hidden_units // LANES), axis=1)
    hidden = (gate_pre * sigmoid(gate_pre) * up_pre * mask).astype(BF16)
    for cut in cuts(model):
        store((gates * dot(hidden, down_ref[:, cut])).astype(BF16), out_refs, cut)


def backward_kernel(count, *refs):
    x_refs, grad_refs = refs[:count], refs[count : 2 * count]
    gate_ref, up_ref, down_ref, router_ref = refs[2 * count : 2 * count + 4]
    out_refs = refs[2 * count + 4 :]
    model, hidden_units = gate_ref.shape
    rows = count * x_refs[0].shape[0]
    gate_pre = jnp.zeros((rows, hidden_units), F32)
    up_pre = jnp.zeros((rows, hidden_units), F32)
    down_slope = jnp.zeros((rows, hidden_units), F32)
    logits = jnp.zeros((rows, LANES), F32)
    for cut in cuts(model):
        x = stacked(x_refs, cut)
        logits += lane_sums(x, router_ref[:, cut])
        down_slope += dot_turned(stacked(grad_refs, cut), down_ref[:, cut])
        gate_pre += dot(x, gate_ref[cut, :])
        up_pre += dot(x, up_ref[cut, :])
    gates = sigmoid(jnp.sum(logits, axis=1, keepdims=True))
    logistic = sigmoid(gate_pre)
    activated = gate_pre * logistic
    down_slope = gates * down_slope
    hidden = (activated * up_pre).astype(BF16).astype(F32)
    weight = jnp.sum(hidden * down_slope, axis=1, keepdims=True) * (1.0 - gates)
    slope = logistic * (1.0 + gate_pre * (1.0 - logistic))
    gate_slope = (down_slope * up_pre * slope).astype(BF16)
    up_slope = (down_slope * activated).astype(BF16)
    for cut in cuts(model):
        through = dot_turned(gate_slope, gate_ref[cut, :])
        through += dot_turned(up_slope, up_ref[cut, :])
        store((through + weight * router_ref[:, cut]).astype(BF16), out_refs, cut)


def bring_kernel(*refs):
    count = len(refs) // 2
    copies = [
        pltpu.make_async_copy(refs[i], refs[count + i], refs[-1].at[i]) for i in range(count)
    ]
    for copy in copies:
        copy.start()
    for copy in copies:
        copy.wait()


def brought_near(*weights):
    return pl.pallas_call(
        bring_kernel,
        in_specs=[pl.BlockSpec(memory_space=pl.ANY)] * len(weights),
        out_specs=[pl.BlockSpec(memory_space=pltpu.VMEM)] * len(weights),
        out_shape=[jax.ShapeDtypeStruct(weight.shape, weight.dtype) for weight in weights],
        scratch_shapes=[pltpu.SemaphoreType.DMA((len(weights),))],
        compiler_params=pltpu.CompilerParams(vmem_limit_bytes=12 * 1024 * 1024),
        cost_estimate=pl.CostEstimate(
            flops=0,
            bytes_accessed=sum(2 * weight.size * weight.dtype.itemsize for weight in weights),
            transcendentals=0,
        ),
    )(*(pltpu.with_memory_space_constraint(weight, pltpu.HBM) for weight in weights))


def expert_parts(pieces, grads, out_rows, gate, up, down, router_row, column_row):
    is_backward = grads is not None
    model, hidden_units = gate.shape
    rows = sum(piece.shape[0] for piece in pieces)
    blocks = [*pieces, *grads] if is_backward else pieces
    last = [router_row] if is_backward else [router_row, column_row]
    operands = [*blocks, gate, up, down, *last]
    products = 5 if is_backward else 3
    return pl.pallas_call(
        functools.partial(backward_kernel if is_backward else forward_kernel, len(pieces)),
        in_specs=[pl.BlockSpec(memory_space=pltpu.VMEM)] * len(operands),
        out_specs=[pl.BlockSpec(memory_space=pltpu.VMEM)] * len(out_rows),
        out_shape=[jax.ShapeDtypeStruct((n, model), BF16) for n in out_rows],
        compiler_params=pltpu.CompilerParams(vmem_limit_bytes=12 * 1024 * 1024),
        cost_estimate=pl.CostEstimate(
            flops=products * 2 * rows * model * hidden_units,
            bytes_accessed=(products * hidden_units + 2 * rows) * model * 2,
            transcendentals=rows * hidden_units,
        ),
    )(*operands)


def on_device(
    forward_in,
    forward_route,
    backward_in,
    backward_route,
    backward_grad,
    router,
    gate_weight,
    up_weight,
    down_weight,
):
    rows = forward_in.shape[1]
    column = lax.axis_index("expert") // (CHIPS * CORES)
    router_row = jnp.where(column == 0, router[0][:, 0], router[0][:, 1]).astype(F32)[None, :]

    column_row = jnp.full((1, LANES), column, F32)

    def split(block, route):
        mine = route[0][:, None] == column
        nothing = jnp.zeros((), block.dtype)
        return jnp.where(mine, block[0], nothing), jnp.where(mine, nothing, block[0])

    def stack(*blocks):
        return jnp.concatenate(blocks, axis=0)

    x_own, x_cross = split(backward_in, backward_route)
    grad_own, grad_cross = split(backward_grad, backward_route)
    lanes = jnp.broadcast_to(forward_route[0].astype(BF16)[:, None], (rows, LANES))
    f0 = jnp.concatenate([forward_in[0], lanes], axis=1)

    x_arrived = other_column(x_cross)
    f0 = after(f0, x_cross)
    f1, f3, f2 = onward(f0), backward(f0), opposite(f0)
    grad_arrived = other_column(grad_cross)
    x0 = stack(x_own, x_arrived)
    x1 = onward(x0)
    early = after(gate_weight[0], x0, router_row, column_row)
    weights = brought_near(early, up_weight[0], down_weight[0])
    here = stack(f0, after(f1, weights[0]), f2, f3)
    crossed = other_column(here)
    g0 = stack(grad_own, after(grad_arrived, here))
    g1 = onward(g0)
    swaps = [other_core(here), other_core(x0), other_core(g0)]
    x2 = onward(after(x1, g0))
    x1_swap, g1_swap = other_core(x1), other_core(g1)
    g2 = onward(after(g1, x1, *swaps))
    x3_from = after(x2, g1, x1_swap)
    x3 = onward(x3_from)
    g3_from = after(g2, x2, g1_swap)
    g3 = onward(g3_from)
    crossed = after(crossed, x3, g3_from)
    pieces = [here, crossed, swaps[0], other_core(crossed)]
    x2_swap, g2_swap = other_core(x2), other_core(g2)
    out_rows = [2 * rows] * CHIPS + [4 * rows] * 2
    parts = expert_parts(pieces, None, out_rows, *weights, router_row, column_row)
    x3_swap = other_core(x3)
    g3, x3_swap, x2_swap, g2_swap, *parts = join(g3, x3_swap, x2_swap, g2_swap, *parts)

    def with_swapped(parts):
        far, near = other_core(parts[CHIPS + 1]), other_core(parts[CHIPS])
        swapped = [near[: 2 * rows], near[2 * rows :], far[: 2 * rows], far[2 * rows :]]
        return list(zip(parts[:CHIPS], swapped))

    def cast(block):
        return block.astype(BF16)

    f_parts = with_swapped(parts)
    f2 = cast(summed(*f_parts[2]))
    xs = [x0, x1, x2, x3, swaps[1], x1_swap, x2_swap, x3_swap]
    gs = [g0, g1, g2, g3, swaps[2], g1_swap, g2_swap, other_core(g3)]
    f2, gs[-1] = join(f2, gs[-1])
    b_parts = expert_parts(xs, gs, out_rows, *weights, router_row, column_row)
    f2_own, f2_cross, *b_parts = join(backward(f2[:rows]), onward(f2[rows:]), *b_parts)

    def with_opposite(parts, own, cross):
        before, later = summed(*parts[1]), summed(*parts[3])
        return (
            cast(stack(before[:rows] + own.astype(F32), before[rows:])),
            cast(stack(later[:rows], later[rows:] + cross.astype(F32))),
        )

    b_parts = with_swapped(b_parts)
    b2 = cast(summed(*b_parts[2]))
    f1, f3 = with_opposite(f_parts, f2_own, f2_cross)
    before, later = backward(stack(b2[:rows], f1)), onward(stack(b2[rows:], f3))
    f1, f3 = before[rows:], later[rows:]
    b1, b3 = with_opposite(b_parts, before[:rows], later[:rows])
    f_home = summed(*f_parts[0], after(f1, b1, b3), f3)
    f_own = cast(f_home[:rows] + forward_in[0].astype(F32))
    f_cross = cast(f_home[rows:])
    b1, b3 = backward(b1), onward(b3)
    b_home = cast(summed(*b_parts[0], after(b1, f_own, f_cross), b3, stack(grad_own, g0[rows:])))
    f_own, f_cross = to_home(f_own, 1, False), to_home(f_cross, 1, True)
    b_own, b_cross = to_home(b_home[:rows], -1, False), to_home(b_home[rows:], -1, True)
    return ((f_own + f_cross)[None], (b_own + b_cross)[None])


def solution(mesh):
    return jax.shard_map(
        on_device,
        mesh=mesh,
        in_specs=(
            P("pipe", "expert", None),
            P("pipe", "expert"),
            P("pipe", "expert", None),
            P("pipe", "expert"),
            P("pipe", "expert", None),
            P("pipe", None, None),
            P("pipe", None, "expert"),
            P("pipe", None, "expert"),
            P("pipe", "expert", None),
        ),
        out_specs=(P("pipe", "expert", None), P("pipe", "expert", None)),
        check_vma=False,
    )
```

```python
import functools

import jax
import jax.numpy as jnp
from jax import lax
from jax.experimental import pallas as pl
from jax.experimental.pallas import tpu as pltpu
from jax.sharding import PartitionSpec as P

COLUMNS = 2
CHIPS = 4
CORES = 2
TILE = 1024
LANES = 128
F32 = jnp.float32
BF16 = jnp.bfloat16


def place(column, chip, core):
    return (column * CHIPS + chip % CHIPS) * CORES + core


def moved(block, step):
    pairs = []
    for column in range(COLUMNS):
        for chip in range(CHIPS):
            for core in range(CORES):
                pairs.append((place(column, chip, core), place(*step(column, chip, core))))
    return lax.ppermute(block, "expert", pairs)


def join(*blocks):
    return lax.optimization_barrier(blocks)


def other_column(block):
    return moved(block, lambda column, chip, core: (1 - column, chip, core))


def other_core(block):
    return moved(block, lambda column, chip, core: (column, chip, 1 - core))


def onward(block):
    return moved(block, lambda column, chip, core: (column, chip + 1 - 2 * core, core))


def backward(block):
    return moved(block, lambda column, chip, core: (column, chip - 1 + 2 * core, core))


def opposite(block):
    return moved(block, lambda column, chip, core: (column, chip + 2, core))


def after(block, *others):
    return lax.optimization_barrier((block, *others))[0]


def to_home(block, distance, cross):
    sections = lax.axis_size("pipe")
    width = COLUMNS * CHIPS * CORES
    pairs = []
    for section in range(sections):
        there = (section + distance) % sections
        for column in range(COLUMNS):
            for chip in range(CHIPS):
                for core in range(CORES):
                    target = 1 - column if cross else column
                    pairs.append(
                        (
                            section * width + place(column, chip, core),
                            there * width + place(target, chip, core),
                        )
                    )
    return lax.ppermute(block, ("pipe", "expert"), pairs)


def summed(mine, *others):
    total = mine.astype(F32)
    for other in others:
        total = total + other.astype(F32)
    return total


def dot(left, right):
    return jnp.dot(left, right, preferred_element_type=F32)


def dot_turned(left, right):
    return lax.dot_general(left, right, (((1,), (1,)), ((), ())), preferred_element_type=F32)


def lane_sums(x, row):
    total = jnp.zeros((x.shape[0], LANES), F32)
    for start in range(0, x.shape[1], LANES):
        part = x[:, start : start + LANES].astype(F32)
        total = total + part * row[:, start : start + LANES]
    return total


def sigmoid(values):
    return 1.0 / (1.0 + jnp.exp(-values))


def cuts(size):
    return [slice(start, start + TILE) for start in range(0, size, TILE)]


def stacked(refs, cut):
    return jnp.concatenate([ref[:, cut] for ref in refs], axis=0)


def interleaved(refs, cut):
    rows = refs[0].shape[0] // CHIPS
    blocks = []
    for own, cross in (refs[:2], refs[2:]):
        for start in range(0, CHIPS * rows, rows):
            blocks.extend([own[start : start + rows, cut], cross[start : start + rows, cut]])
    return jnp.concatenate(blocks, axis=0)


def store(part, out_refs, cut):
    start = 0
    for ref in out_refs:
        rows = ref.shape[0]
        ref[:, cut] = part[start : start + rows]
        start += rows


def forward_kernel(count, *refs):
    x_refs = refs[:count]
    gate_ref, up_ref, down_ref, router_ref, column_ref = refs[count : count + 5]
    out_refs = refs[count + 5 :]
    model, hidden_units = gate_ref.shape
    rows = count * x_refs[0].shape[0]
    gate_pre = jnp.zeros((rows, hidden_units), F32)
    up_pre = jnp.zeros((rows, hidden_units), F32)
    logits = jnp.zeros((rows, LANES), F32)
    for cut in cuts(model):
        x = interleaved(x_refs, cut)
        logits += lane_sums(x, router_ref[:, cut])
        gate_pre += dot(x, gate_ref[cut, :])
        up_pre += dot(x, up_ref[cut, :])
    gates = sigmoid(jnp.sum(logits, axis=1, keepdims=True))
    routes = interleaved(x_refs, slice(model, model + LANES)).astype(F32)
    mask = (routes == column_ref[...]).astype(F32)
    mask = jnp.concatenate([mask] * (hidden_units // LANES), axis=1)
    hidden = (gate_pre * sigmoid(gate_pre) * up_pre * mask).astype(BF16)
    for cut in cuts(model):
        store((gates * dot(hidden, down_ref[:, cut])).astype(BF16), out_refs, cut)


def gate_and_up_kernel(count, *refs):
    x_refs = refs[:count]
    gate_ref, up_ref, router_ref, gate_pre_ref, up_pre_ref, gates_ref = refs[count:]
    model, hidden_units = gate_ref.shape
    rows = gate_pre_ref.shape[0]
    gate_pre = jnp.zeros((rows, hidden_units), F32)
    up_pre = jnp.zeros((rows, hidden_units), F32)
    logits = jnp.zeros((rows, LANES), F32)
    for cut in cuts(model):
        x = stacked(x_refs, cut)
        logits += lane_sums(x, router_ref[:, cut])
        gate_pre += dot(x, gate_ref[cut, :])
        up_pre += dot(x, up_ref[cut, :])
    gate_pre_ref[...] = gate_pre
    up_pre_ref[...] = up_pre
    gates = sigmoid(jnp.sum(logits, axis=1, keepdims=True))
    gates_ref[...] = jnp.broadcast_to(gates, gates_ref.shape)


def backward_kernel(count, *refs):
    grad_refs = refs[:count]
    gate_pre_ref, up_pre_ref, gates_ref = refs[count : count + 3]
    gate_ref, up_ref, down_ref, router_ref = refs[count + 3 : count + 7]
    out_refs = refs[count + 7 :]
    model, hidden_units = gate_ref.shape
    down_slope = jnp.zeros(gate_pre_ref.shape, F32)
    for cut in cuts(model):
        down_slope += dot_turned(stacked(grad_refs, cut), down_ref[:, cut])
    gates = gates_ref[:, :1]
    gate_pre = gate_pre_ref[...]
    up_pre = up_pre_ref[...]
    logistic = sigmoid(gate_pre)
    activated = gate_pre * logistic
    down_slope = gates * down_slope
    hidden = (activated * up_pre).astype(BF16).astype(F32)
    weight = jnp.sum(hidden * down_slope, axis=1, keepdims=True) * (1.0 - gates)
    slope = logistic * (1.0 + gate_pre * (1.0 - logistic))
    gate_slope = (down_slope * up_pre * slope).astype(BF16)
    up_slope = (down_slope * activated).astype(BF16)
    for cut in cuts(model):
        through = dot_turned(gate_slope, gate_ref[cut, :])
        through += dot_turned(up_slope, up_ref[cut, :])
        store((through + weight * router_ref[:, cut]).astype(BF16), out_refs, cut)


def fetch(pairs, semaphores):
    copies = [
        pltpu.make_async_copy(source, target, semaphores.at[i])
        for i, (source, target) in enumerate(pairs)
    ]
    for copy in copies:
        copy.start()
    for copy in copies:
        copy.wait()


def upright(row):
    count = row.shape[1]
    on_diagonal = (
        lax.broadcasted_iota(jnp.int32, (count, count), 0)
        == lax.broadcasted_iota(jnp.int32, (count, count), 1)
    ).astype(F32)
    return jnp.sum(on_diagonal * row.astype(F32), axis=1, keepdims=True)


def this_column():
    return (lax.axis_index("expert") // (CHIPS * CORES)).astype(F32)


def part_kernel(route_hbm, x_hbm, grad_hbm, *refs):
    x_own_ref, x_cross_ref, grad_own_ref, grad_cross_ref = refs[:4]
    route_ref, x_ref, grad_ref, semaphores = refs[4:]
    fetch([(route_hbm, route_ref), (x_hbm, x_ref), (grad_hbm, grad_ref)], semaphores)
    mine = (upright(route_ref[...]) == this_column()).astype(F32)
    for ref, own_ref, cross_ref in (
        (x_ref, x_own_ref, x_cross_ref),
        (grad_ref, grad_own_ref, grad_cross_ref),
    ):
        block = ref[...].astype(F32)
        own_ref[...] = (block * mine).astype(BF16)
        cross_ref[...] = (block * (1.0 - mine)).astype(BF16)


def mark_kernel(route_hbm, rows_hbm, router_hbm, *refs):
    rows_ref, router_row_ref, column_ref, route_ref, plain_ref, router_ref, semaphores = refs
    fetch([(route_hbm, route_ref), (rows_hbm, plain_ref), (router_hbm, router_ref)], semaphores)
    model = plain_ref.shape[1]
    rows_ref[:, :model] = plain_ref[...]
    lanes = jnp.broadcast_to(upright(route_ref[...]), (plain_ref.shape[0], LANES))
    rows_ref[:, model:] = lanes.astype(BF16)
    column = this_column()
    both = router_ref[...].astype(F32)
    router_row_ref[...] = both[:1] * (1.0 - column) + both[1:] * column
    column_ref[...] = jnp.broadcast_to(column, column_ref.shape)


def from_hbm(body, operands, results):
    return pl.pallas_call(
        body,
        in_specs=[pl.BlockSpec(memory_space=pl.ANY)] * len(operands),
        out_specs=[pl.BlockSpec(memory_space=pltpu.VMEM)] * len(results),
        out_shape=results,
        scratch_shapes=[
            *[pltpu.VMEM(operand.shape, operand.dtype) for operand in operands],
            pltpu.SemaphoreType.DMA((len(operands),)),
        ],
        compiler_params=pltpu.CompilerParams(vmem_limit_bytes=12 * 1024 * 1024),
    )(*(pltpu.with_memory_space_constraint(operand, pltpu.HBM) for operand in operands))


def bring_kernel(*refs):
    count = len(refs) // 2
    fetch(list(zip(refs[:count], refs[count : 2 * count])), refs[-1])


def brought_near(*weights):
    return pl.pallas_call(
        bring_kernel,
        in_specs=[pl.BlockSpec(memory_space=pl.ANY)] * len(weights),
        out_specs=[pl.BlockSpec(memory_space=pltpu.VMEM)] * len(weights),
        out_shape=[jax.ShapeDtypeStruct(weight.shape, weight.dtype) for weight in weights],
        scratch_shapes=[pltpu.SemaphoreType.DMA((len(weights),))],
        compiler_params=pltpu.CompilerParams(vmem_limit_bytes=12 * 1024 * 1024),
        cost_estimate=pl.CostEstimate(
            flops=0,
            bytes_accessed=sum(2 * weight.size * weight.dtype.itemsize for weight in weights),
            transcendentals=0,
        ),
    )(*(pltpu.with_memory_space_constraint(weight, pltpu.HBM) for weight in weights))


def in_vmem(body, operands, results, products):
    model, hidden_units = max(x.shape[0] for x in operands), LANES * 2
    rows = sum(x.shape[0] for x in results[:8]) if len(results) > 3 else results[0].shape[0]
    here = pl.BlockSpec(memory_space=pltpu.VMEM)
    return pl.pallas_call(
        body,
        in_specs=[here] * len(operands),
        out_specs=[here] * len(results),
        out_shape=results,
        compiler_params=pltpu.CompilerParams(vmem_limit_bytes=12 * 1024 * 1024),
        cost_estimate=pl.CostEstimate(
            flops=products * 2 * rows * model * hidden_units,
            bytes_accessed=(products * hidden_units + 2 * rows) * model * 2,
            transcendentals=rows * hidden_units,
        ),
    )(*operands)


def part_shapes(out_rows, model):
    return [jax.ShapeDtypeStruct((rows, model), BF16) for rows in out_rows]


def forward_parts(pieces, out_rows, gate, up, down, router_row, column_row):
    body = functools.partial(forward_kernel, len(pieces))
    operands = [*pieces, gate, up, down, router_row, column_row]
    return in_vmem(body, operands, part_shapes(out_rows, gate.shape[0]), 3)


def gate_and_up(pieces, gate, up, router_row):
    rows = sum(piece.shape[0] for piece in pieces)
    body = functools.partial(gate_and_up_kernel, len(pieces))
    shapes = [(rows, gate.shape[1]), (rows, gate.shape[1]), (rows, LANES)]
    results = [jax.ShapeDtypeStruct(shape, F32) for shape in shapes]
    return in_vmem(body, [*pieces, gate, up, router_row], results, 2)


def backward_parts(grads, pre, out_rows, gate, up, down, router_row):
    body = functools.partial(backward_kernel, len(grads))
    operands = [*grads, *pre, gate, up, down, router_row]
    return in_vmem(body, operands, part_shapes(out_rows, gate.shape[0]), 3)


def on_device(
    forward_in,
    forward_route,
    backward_in,
    backward_route,
    backward_grad,
    router,
    gate_weight,
    up_weight,
    down_weight,
):
    rows = forward_in.shape[1]
    model = forward_in.shape[2]
    block = jax.ShapeDtypeStruct((rows, model), BF16)
    x_own, x_cross, grad_own, grad_cross = from_hbm(
        part_kernel, [backward_route, backward_in[0], backward_grad[0]], [block] * 4
    )
    marked = [
        jax.ShapeDtypeStruct((rows, model + LANES), BF16),
        jax.ShapeDtypeStruct((1, model), F32),
        jax.ShapeDtypeStruct((1, LANES), F32),
    ]
    f0, router_row, column_row = from_hbm(
        mark_kernel, [after(forward_route, x_cross), forward_in[0], router[0].T], marked
    )

    def stack(*blocks):
        return jnp.concatenate(blocks, axis=0)

    x_arrived = other_column(x_cross)
    f1, f3, f2 = onward(f0), backward(f0), opposite(f0)
    grad_arrived = other_column(grad_cross)
    x0 = stack(x_own, x_arrived)
    x1 = onward(x0)
    early = after(gate_weight[0], x0)
    weights = brought_near(early, up_weight[0], down_weight[0])
    here = stack(f0, after(f1, weights[0]), f2, f3)
    crossed = other_column(here)
    g0 = stack(grad_own, after(grad_arrived, here))
    g1 = onward(g0)
    swaps = [other_core(here), other_core(x0), other_core(g0)]
    x2 = onward(after(x1, g0))
    x1_swap, g1_swap = other_core(x1), other_core(g1)
    g2 = onward(after(g1, x1, *swaps))
    x3_from = after(x2, g1, x1_swap)
    x3 = onward(x3_from)
    g3_from = after(g2, x2, g1_swap)
    g3 = onward(g3_from)
    crossed = after(crossed, x3, g3_from)
    pieces = [here, crossed, swaps[0], other_core(crossed)]
    x2_swap, g2_swap = other_core(x2), other_core(g2)
    out_rows = [2 * rows] * (2 * CHIPS)
    parts = forward_parts(pieces, out_rows, *weights, router_row, column_row)
    xs = [x0, x1, x2, x3, swaps[1], x1_swap, x2_swap, other_core(x3)]
    xs[0] = after(xs[0], parts[0])
    pre = gate_and_up(xs, weights[0], weights[1], router_row)
    far, far_other = parts[2], parts[CHIPS + 2]
    g3, g2_swap, *parts = join(g3, g2_swap, *pre, *parts)
    pre, parts = parts[:3], parts[3:]
    parts[2], parts[CHIPS + 2] = far, far_other

    def with_swapped(parts):
        swapped = []
        for block in map(other_core, parts[CHIPS:]):
            swapped.extend(jnp.split(block, block.shape[0] // (2 * rows)))
        return list(zip(parts[:CHIPS], swapped))

    def cast(block):
        return block.astype(BF16)

    f_parts = with_swapped(parts)
    f2 = cast(summed(*f_parts[2]))
    gs = [g0, g1, g2, g3, swaps[2], g1_swap, g2_swap, other_core(g3)]
    f2, gs[-1] = join(f2, gs[-1])
    out_rows = [2 * rows] * (CHIPS + 1) + [2 * rows * (CHIPS - 1)]
    b_parts = backward_parts(gs, pre, out_rows, *weights, router_row)
    f2_own, f2_cross, *b_parts = join(backward(f2[:rows]), onward(f2[rows:]), *b_parts)

    f_before, f_later = summed(*f_parts[1]), summed(*f_parts[3])
    f1 = backward(cast(stack(f_before[:rows] + f2_own.astype(F32), f_before[rows:])))
    f3 = onward(cast(stack(f_later[:rows], f_later[rows:] + f2_cross.astype(F32))))

    b_parts = with_swapped(b_parts)
    b2 = cast(summed(*b_parts[2]))
    b_before, b_later = summed(*b_parts[1]), summed(*b_parts[3])
    before = backward(stack(b2[:rows], cast(b_before[rows:])))
    later = onward(stack(b2[rows:], cast(b_later[:rows])))
    b1 = cast(b_before[:rows] + before[:rows].astype(F32))
    b3 = cast(b_later[rows:] + later[:rows].astype(F32))
    f1 = after(f1, b1, b3)
    b1, b3 = backward(b1), onward(b3)
    f_home = summed(*f_parts[0], f1, f3)
    f_own = cast(f_home[:rows] + forward_in[0].astype(F32))
    f_cross = cast(f_home[rows:])
    b1 = after(b1, f_own, f_cross)
    b_home = summed(*b_parts[0], stack(grad_own, g0[rows:]))
    b_own = cast(summed(b_home[:rows], b1, later[rows:]))
    b_cross = cast(summed(b_home[rows:], before[rows:], b3))
    f_own, f_cross = to_home(f_own, 1, False), to_home(f_cross, 1, True)
    b_own, b_cross = to_home(b_own, -1, False), to_home(b_cross, -1, True)
    return ((f_own + f_cross)[None], (b_own + b_cross)[None])


def solution(mesh):
    return jax.shard_map(
        on_device,
        mesh=mesh,
        in_specs=(
            P("pipe", "expert", None),
            P("pipe", "expert"),
            P("pipe", "expert", None),
            P("pipe", "expert"),
            P("pipe", "expert", None),
            P("pipe", None, None),
            P("pipe", None, "expert"),
            P("pipe", None, "expert"),
            P("pipe", "expert", None),
        ),
        out_specs=(P("pipe", "expert", None), P("pipe", "expert", None)),
        check_vma=False,
    )
```

```python
import functools

import jax
import jax.numpy as jnp
from jax import lax
from jax.experimental import pallas as pl
from jax.experimental.pallas import tpu as pltpu
from jax.sharding import PartitionSpec as P

COLUMNS = 2
CHIPS = 4
CORES = 2
TILE = 1024
LANES = 128
F32 = jnp.float32
BF16 = jnp.bfloat16


def place(column, chip, core):
    return (column * CHIPS + chip % CHIPS) * CORES + core


def moved(block, step):
    pairs = []
    for column in range(COLUMNS):
        for chip in range(CHIPS):
            for core in range(CORES):
                pairs.append((place(column, chip, core), place(*step(column, chip, core))))
    return lax.ppermute(block, "expert", pairs)


def join(*blocks):
    return lax.optimization_barrier(blocks)


def other_column(block):
    return moved(block, lambda column, chip, core: (1 - column, chip, core))


def other_core(block):
    return moved(block, lambda column, chip, core: (column, chip, 1 - core))


def onward(block):
    return moved(block, lambda column, chip, core: (column, chip + 1 - 2 * core, core))


def backward(block):
    return moved(block, lambda column, chip, core: (column, chip - 1 + 2 * core, core))


def opposite(block):
    return moved(block, lambda column, chip, core: (column, chip + 2, core))


def after(block, *others):
    return lax.optimization_barrier((block, *others))[0]


def to_home(block, distance, cross):
    sections = lax.axis_size("pipe")
    width = COLUMNS * CHIPS * CORES
    pairs = []
    for section in range(sections):
        there = (section + distance) % sections
        for column in range(COLUMNS):
            for chip in range(CHIPS):
                for core in range(CORES):
                    target = 1 - column if cross else column
                    pairs.append(
                        (
                            section * width + place(column, chip, core),
                            there * width + place(target, chip, core),
                        )
                    )
    return lax.ppermute(block, ("pipe", "expert"), pairs)


def summed(mine, *others):
    total = mine.astype(F32)
    for other in others:
        total = total + other.astype(F32)
    return total


def dot(left, right):
    return jnp.dot(left, right, preferred_element_type=F32)


def dot_turned(left, right):
    return lax.dot_general(left, right, (((1,), (1,)), ((), ())), preferred_element_type=F32)


def lane_sums(x, row):
    total = jnp.zeros((x.shape[0], LANES), F32)
    for start in range(0, x.shape[1], LANES):
        part = x[:, start : start + LANES].astype(F32)
        total = total + part * row[:, start : start + LANES]
    return total


def sigmoid(values):
    return 1.0 / (1.0 + jnp.exp(-values))


def cuts(size):
    return [slice(start, start + TILE) for start in range(0, size, TILE)]


def stacked(refs, cut):
    return jnp.concatenate([ref[:, cut] for ref in refs], axis=0)


def interleaved(refs, cut):
    rows = refs[0].shape[0] // CHIPS
    blocks = []
    for own, cross in (refs[:2], refs[2:]):
        for start in range(0, CHIPS * rows, rows):
            blocks.extend([own[start : start + rows, cut], cross[start : start + rows, cut]])
    return jnp.concatenate(blocks, axis=0)


def store(part, out_refs, cut):
    start = 0
    for ref in out_refs:
        rows = ref.shape[0]
        ref[:, cut] = part[start : start + rows]
        start += rows


def forward_kernel(count, *refs):
    x_refs = refs[:count]
    gate_ref, up_ref, down_ref, router_ref, column_ref = refs[count : count + 5]
    out_refs = refs[count + 5 :]
    model, hidden_units = gate_ref.shape
    rows = count * x_refs[0].shape[0]
    gate_pre = jnp.zeros((rows, hidden_units), F32)
    up_pre = jnp.zeros((rows, hidden_units), F32)
    logits = jnp.zeros((rows, LANES), F32)
    for cut in cuts(model):
        x = interleaved(x_refs, cut)
        logits += lane_sums(x, router_ref[:, cut])
        gate_pre += dot(x, gate_ref[cut, :])
        up_pre += dot(x, up_ref[cut, :])
    gates = sigmoid(jnp.sum(logits, axis=1, keepdims=True))
    routes = interleaved(x_refs, slice(model, model + LANES)).astype(F32)
    mask = (routes == column_ref[...]).astype(F32)
    mask = jnp.concatenate([mask] * (hidden_units // LANES), axis=1)
    hidden = (gate_pre * sigmoid(gate_pre) * up_pre * mask).astype(BF16)

    @pl.loop(0, model // TILE)
    def _(n):
        cut = pl.ds(pl.multiple_of(n * TILE, TILE), TILE)
        store((gates * dot(hidden, down_ref[:, cut])).astype(BF16), out_refs, cut)


def gate_and_up_kernel(count, *refs):
    x_refs = refs[:count]
    gate_ref, up_ref, router_ref, gate_pre_ref, up_pre_ref, gates_ref = refs[count:]
    model, hidden_units = gate_ref.shape
    rows = gate_pre_ref.shape[0]
    gate_pre = jnp.zeros((rows, hidden_units), F32)
    up_pre = jnp.zeros((rows, hidden_units), F32)
    logits = jnp.zeros((rows, LANES), F32)
    for cut in cuts(model):
        x = stacked(x_refs, cut)
        logits += lane_sums(x, router_ref[:, cut])
        gate_pre += dot(x, gate_ref[cut, :])
        up_pre += dot(x, up_ref[cut, :])
    gate_pre_ref[...] = gate_pre
    up_pre_ref[...] = up_pre
    gates = sigmoid(jnp.sum(logits, axis=1, keepdims=True))
    gates_ref[...] = jnp.broadcast_to(gates, gates_ref.shape)


def backward_kernel(count, *refs):
    grad_refs = refs[:count]
    gate_pre_ref, up_pre_ref, gates_ref = refs[count : count + 3]
    gate_ref, up_ref, down_ref, router_ref = refs[count + 3 : count + 7]
    out_refs = refs[count + 7 :]
    model, hidden_units = gate_ref.shape
    down_slope = jnp.zeros(gate_pre_ref.shape, F32)
    for cut in cuts(model):
        down_slope += dot_turned(stacked(grad_refs, cut), down_ref[:, cut])
    gates = gates_ref[:, :1]
    gate_pre = gate_pre_ref[...]
    up_pre = up_pre_ref[...]
    logistic = sigmoid(gate_pre)
    activated = gate_pre * logistic
    down_slope = gates * down_slope
    hidden = (activated * up_pre).astype(BF16).astype(F32)
    weight = jnp.sum(hidden * down_slope, axis=1, keepdims=True) * (1.0 - gates)
    slope = logistic * (1.0 + gate_pre * (1.0 - logistic))
    gate_slope = (down_slope * up_pre * slope).astype(BF16)
    up_slope = (down_slope * activated).astype(BF16)

    @pl.loop(0, model // TILE)
    def _(n):
        cut = pl.ds(pl.multiple_of(n * TILE, TILE), TILE)
        through = dot_turned(gate_slope, gate_ref[cut, :])
        through += dot_turned(up_slope, up_ref[cut, :])
        store((through + weight * router_ref[:, cut]).astype(BF16), out_refs, cut)


def fetch(pairs, semaphores):
    copies = [
        pltpu.make_async_copy(source, target, semaphores.at[i])
        for i, (source, target) in enumerate(pairs)
    ]
    for copy in copies:
        copy.start()
    for copy in copies:
        copy.wait()


def upright(row):
    count = row.shape[1]
    on_diagonal = (
        lax.broadcasted_iota(jnp.int32, (count, count), 0)
        == lax.broadcasted_iota(jnp.int32, (count, count), 1)
    ).astype(F32)
    return jnp.sum(on_diagonal * row.astype(F32), axis=1, keepdims=True)


def this_column():
    return (lax.axis_index("expert") // (CHIPS * CORES)).astype(F32)


def part_kernel(route_hbm, x_hbm, grad_hbm, *refs):
    x_own_ref, x_cross_ref, grad_own_ref, grad_cross_ref = refs[:4]
    route_ref, x_ref, grad_ref, semaphores = refs[4:]
    fetch([(route_hbm, route_ref), (x_hbm, x_ref), (grad_hbm, grad_ref)], semaphores)
    mine = (upright(route_ref[...]) == this_column()).astype(F32)
    for ref, own_ref, cross_ref in (
        (x_ref, x_own_ref, x_cross_ref),
        (grad_ref, grad_own_ref, grad_cross_ref),
    ):
        block = ref[...].astype(F32)
        own_ref[...] = (block * mine).astype(BF16)
        cross_ref[...] = (block * (1.0 - mine)).astype(BF16)


def mark_kernel(route_hbm, rows_hbm, router_hbm, *refs):
    rows_ref, router_row_ref, column_ref, route_ref, plain_ref, router_ref, semaphores = refs
    fetch([(route_hbm, route_ref), (rows_hbm, plain_ref), (router_hbm, router_ref)], semaphores)
    model = plain_ref.shape[1]
    rows_ref[:, :model] = plain_ref[...]
    lanes = jnp.broadcast_to(upright(route_ref[...]), (plain_ref.shape[0], LANES))
    rows_ref[:, model:] = lanes.astype(BF16)
    column = this_column()
    both = router_ref[...].astype(F32)
    router_row_ref[...] = both[:1] * (1.0 - column) + both[1:] * column
    column_ref[...] = jnp.broadcast_to(column, column_ref.shape)


def from_hbm(body, operands, results):
    return pl.pallas_call(
        body,
        in_specs=[pl.BlockSpec(memory_space=pl.ANY)] * len(operands),
        out_specs=[pl.BlockSpec(memory_space=pltpu.VMEM)] * len(results),
        out_shape=results,
        scratch_shapes=[
            *[pltpu.VMEM(operand.shape, operand.dtype) for operand in operands],
            pltpu.SemaphoreType.DMA((len(operands),)),
        ],
        compiler_params=pltpu.CompilerParams(vmem_limit_bytes=12 * 1024 * 1024),
    )(*(pltpu.with_memory_space_constraint(operand, pltpu.HBM) for operand in operands))


def bring_kernel(*refs):
    count = len(refs) // 2
    fetch(list(zip(refs[:count], refs[count : 2 * count])), refs[-1])


def brought_near(*weights):
    return pl.pallas_call(
        bring_kernel,
        in_specs=[pl.BlockSpec(memory_space=pl.ANY)] * len(weights),
        out_specs=[pl.BlockSpec(memory_space=pltpu.VMEM)] * len(weights),
        out_shape=[jax.ShapeDtypeStruct(weight.shape, weight.dtype) for weight in weights],
        scratch_shapes=[pltpu.SemaphoreType.DMA((len(weights),))],
        compiler_params=pltpu.CompilerParams(vmem_limit_bytes=12 * 1024 * 1024),
        cost_estimate=pl.CostEstimate(
            flops=0,
            bytes_accessed=sum(2 * weight.size * weight.dtype.itemsize for weight in weights),
            transcendentals=0,
        ),
    )(*(pltpu.with_memory_space_constraint(weight, pltpu.HBM) for weight in weights))


def in_vmem(body, operands, results, products):
    model, hidden_units = max(x.shape[0] for x in operands), LANES * 2
    rows = sum(x.shape[0] for x in results[:8]) if len(results) > 3 else results[0].shape[0]
    here = pl.BlockSpec(memory_space=pltpu.VMEM)
    return pl.pallas_call(
        body,
        in_specs=[here] * len(operands),
        out_specs=[here] * len(results),
        out_shape=results,
        compiler_params=pltpu.CompilerParams(vmem_limit_bytes=12 * 1024 * 1024),
        cost_estimate=pl.CostEstimate(
            flops=products * 2 * rows * model * hidden_units,
            bytes_accessed=(products * hidden_units + 2 * rows) * model * 2,
            transcendentals=rows * hidden_units,
        ),
    )(*operands)


def part_shapes(out_rows, model):
    return [jax.ShapeDtypeStruct((rows, model), BF16) for rows in out_rows]


def forward_parts(pieces, out_rows, gate, up, down, router_row, column_row):
    body = functools.partial(forward_kernel, len(pieces))
    operands = [*pieces, gate, up, down, router_row, column_row]
    return in_vmem(body, operands, part_shapes(out_rows, gate.shape[0]), 3)


def gate_and_up(pieces, gate, up, router_row):
    rows = sum(piece.shape[0] for piece in pieces)
    body = functools.partial(gate_and_up_kernel, len(pieces))
    shapes = [(rows, gate.shape[1]), (rows, gate.shape[1]), (rows, LANES)]
    results = [jax.ShapeDtypeStruct(shape, F32) for shape in shapes]
    return in_vmem(body, [*pieces, gate, up, router_row], results, 2)


def backward_parts(grads, pre, out_rows, gate, up, down, router_row):
    body = functools.partial(backward_kernel, len(grads))
    operands = [*grads, *pre, gate, up, down, router_row]
    return in_vmem(body, operands, part_shapes(out_rows, gate.shape[0]), 3)


def on_device(
    forward_in,
    forward_route,
    backward_in,
    backward_route,
    backward_grad,
    router,
    gate_weight,
    up_weight,
    down_weight,
):
    rows = forward_in.shape[1]
    model = forward_in.shape[2]
    block = jax.ShapeDtypeStruct((rows, model), BF16)
    x_own, x_cross, grad_own, grad_cross = from_hbm(
        part_kernel, [backward_route, backward_in[0], backward_grad[0]], [block] * 4
    )
    marked = [
        jax.ShapeDtypeStruct((rows, model + LANES), BF16),
        jax.ShapeDtypeStruct((1, model), F32),
        jax.ShapeDtypeStruct((1, LANES), F32),
    ]
    f0, router_row, column_row = from_hbm(
        mark_kernel, [after(forward_route, x_cross), forward_in[0], router[0].T], marked
    )

    def stack(*blocks):
        return jnp.concatenate(blocks, axis=0)

    x_arrived = other_column(x_cross)
    f1, f3, f2 = onward(f0), backward(f0), opposite(f0)
    grad_arrived = other_column(grad_cross)
    x0 = stack(x_own, x_arrived)
    x1 = onward(x0)
    early = after(gate_weight[0], x0)
    weights = brought_near(early, up_weight[0], down_weight[0])
    here = stack(f0, after(f1, weights[0]), f2, f3)
    crossed = other_column(here)
    g0 = stack(grad_own, after(grad_arrived, here))
    g1 = onward(g0)
    swaps = [other_core(here), other_core(x0), other_core(g0)]
    x2 = onward(after(x1, g0))
    x1_swap, g1_swap = other_core(x1), other_core(g1)
    g2 = onward(after(g1, x1, *swaps))
    x3_from = after(x2, g1, x1_swap)
    x3 = onward(x3_from)
    g3_from = after(g2, x2, g1_swap)
    g3 = onward(g3_from)
    crossed = after(crossed, x3, g3_from)
    pieces = [here, crossed, swaps[0], other_core(crossed)]
    x2_swap, g2_swap = other_core(x2), other_core(g2)
    out_rows = [2 * rows] * (2 * CHIPS)
    parts = forward_parts(pieces, out_rows, *weights, router_row, column_row)
    xs = [x0, x1, x2, x3, swaps[1], x1_swap, x2_swap, other_core(x3)]
    xs[0] = after(xs[0], parts[0])
    pre = gate_and_up(xs, weights[0], weights[1], router_row)
    far, far_other = parts[2], parts[CHIPS + 2]
    g3, g2_swap, *parts = join(g3, g2_swap, *pre, *parts)
    pre, parts = parts[:3], parts[3:]
    parts[2], parts[CHIPS + 2] = far, far_other

    def with_swapped(parts):
        swapped = []
        for block in map(other_core, parts[CHIPS:]):
            swapped.extend(jnp.split(block, block.shape[0] // (2 * rows)))
        return list(zip(parts[:CHIPS], swapped))

    def cast(block):
        return block.astype(BF16)

    f_parts = with_swapped(parts)
    f2 = cast(summed(*f_parts[2]))
    gs = [g0, g1, g2, g3, swaps[2], g1_swap, g2_swap, other_core(g3)]
    f2, gs[-1] = join(f2, gs[-1])
    out_rows = [2 * rows] * (CHIPS + 1) + [2 * rows * (CHIPS - 1)]
    b_parts = backward_parts(gs, pre, out_rows, *weights, router_row)
    f2_own, f2_cross, *b_parts = join(backward(f2[:rows]), onward(f2[rows:]), *b_parts)

    f_before, f_later = summed(*f_parts[1]), summed(*f_parts[3])
    f1 = backward(cast(stack(f_before[:rows] + f2_own.astype(F32), f_before[rows:])))
    f3 = onward(cast(stack(f_later[:rows], f_later[rows:] + f2_cross.astype(F32))))

    b_parts = with_swapped(b_parts)
    b2 = cast(summed(*b_parts[2]))
    b_before, b_later = summed(*b_parts[1]), summed(*b_parts[3])
    before = backward(stack(b2[:rows], cast(b_before[rows:])))
    later = onward(stack(b2[rows:], cast(b_later[:rows])))
    b1 = cast(b_before[:rows] + before[:rows].astype(F32))
    b3 = cast(b_later[rows:] + later[:rows].astype(F32))
    f1 = after(f1, b1, b3)
    b1, b3 = backward(b1), onward(b3)
    f_home = summed(*f_parts[0], f1, f3)
    f_own = cast(f_home[:rows] + forward_in[0].astype(F32))
    f_cross = cast(f_home[rows:])
    b1 = after(b1, f_own, f_cross)
    b_home = summed(*b_parts[0], stack(grad_own, g0[rows:]))
    b_own = cast(summed(b_home[:rows], b1, later[rows:]))
    b_cross = cast(summed(b_home[rows:], before[rows:], b3))
    f_own, f_cross = to_home(f_own, 1, False), to_home(f_cross, 1, True)
    b_own, b_cross = to_home(b_own, -1, False), to_home(b_cross, -1, True)
    return ((f_own + f_cross)[None], (b_own + b_cross)[None])


def solution(mesh):
    return jax.shard_map(
        on_device,
        mesh=mesh,
        in_specs=(
            P("pipe", "expert", None),
            P("pipe", "expert"),
            P("pipe", "expert", None),
            P("pipe", "expert"),
            P("pipe", "expert", None),
            P("pipe", None, None),
            P("pipe", None, "expert"),
            P("pipe", None, "expert"),
            P("pipe", "expert", None),
        ),
        out_specs=(P("pipe", "expert", None), P("pipe", "expert", None)),
        check_vma=False,
    )
```
